512 devices in a mesh: seq: 32 (over x, z), head: 16 (over y, core).
Axes of the slice: x: 4, y: 8, z: 8, core: 2. Of those that a mesh axis runs over, the one named last changes fastest.
Arguments:
- queries: bfloat16 [32768, 16, 128], P('seq', 'head'), may hold values from -6 to 6
- keys: bfloat16 [32768, 16, 128], P('seq', 'head'), may hold values from -0.26516504 to 0.26516504
- values: bfloat16 [32768, 16, 128], P('seq', 'head'), may hold values from -6 to 6
- key_gain: float32 [16, 128], P('head'), may hold values from 0.25 to 2.5
- reg: float32 [16], P('head'), may hold values from 0.5 to 4
- norm_gain: float32 [16, 128], P('head'), may hold values from 0.5 to 1.5
- out_weight: bfloat16 [2048, 2048], P('head'), may hold values from -0.1875 to 0.1875
Outputs:
- mixed: bfloat16 [32768, 2048], P('seq', 'head')
The draws below stay inside these ranges and needn't reach their ends.
All inputs are finite; a program needn't handle non-finite values.
Results may differ from the reference program's by a relative error of at most 0.0058.
Values sent between devices are 32-bit elements; how exact they have to be, the bound alone decides.
No kernel may reach another device: no remote copies, remote signals or barrier semaphores. Data moves between devices by JAX's collectives and lax.ppermute only.
A program may use at most 64 MiB of HBM per device.

```python
import math
import jax
import jax.numpy as jnp
from jax import lax

D = 2048
DH = 128
TOK_DEV = 1024
ITERS = 15
HEADS = 16
TOKENS = 32768


def draw_keys(key, part):
    key = jax.random.fold_in(key, 11)
    spread = 0.5 * DH ** (-0.5)
    sample = jax.random.normal(key, (TOKENS, HEADS, DH), jnp.float32)
    return (jnp.clip(sample, -6.0, 6.0) * spread).astype(jnp.bfloat16)


def spiked(result, own_key, source, target, shards_of, factor):
    owner, partner = [(jnp.arange(result.shape[position]) // (result.shape[position] // shards_of)).reshape([-1 if axis == position else 1 for axis in range(result.ndim)]) for position in (source, target)]
    chosen = jax.random.permutation(own_key, shards_of)[partner]
    strong = (owner == chosen) | (owner == (partner + shards_of // 2) % shards_of)
    return jnp.where(strong, factor * result, result)


def steps_of(key, dims, pieces, low, largest):
    loudness, own = 1.0, jax.random.fold_in(key, 6)
    for position, blocks in pieces:
        steps = jnp.exp(jax.random.uniform(jax.random.fold_in(own, position), (blocks,), jnp.float32, low / len(pieces), largest / len(pieces)))
        loudness = loudness * jnp.repeat(steps, dims[position] // blocks).reshape([-1 if axis == position else 1 for axis in range(len(dims))])
    return loudness


def gaussian(key, shape, scale, bound, shards=(), kind=jnp.bfloat16):
    values = scale * jax.random.normal(key, shape, jnp.float32)
    if shards:
        values = values * steps_of(key, shape, shards, -0.22, 0.18)
    return jnp.clip(values, -bound, bound).astype(kind)


def noise_with(rng, extent, deviation, reach, shards, heavy, held_as=jnp.bfloat16):
    values = deviation * jax.random.normal(rng, extent, jnp.float32)
    if shards:
        values = values * steps_of(rng, extent, shards, -0.22, 0.18)
    return jnp.clip(spiked(values, jax.random.fold_in(rng, 3), *heavy), -reach, reach).astype(held_as)


def setup_inputs(seed: int = 0) -> dict:
    arg_keys = jax.random.split(jax.random.key(seed), 8)
    queries = gaussian(arg_keys[0], (TOKENS, HEADS, DH), 1.0, 6.0, ((0, 32), (1, 16)))
    keys = draw_keys(jax.random.fold_in(arg_keys[7], 71), 0)
    values = gaussian(arg_keys[2], (TOKENS, HEADS, DH), 1.0, 6.0, ((0, 32), (1, 16)))
    key_gain = jnp.clip(jnp.exp(math.log(2.5) - 2.3025851 * jax.random.uniform(arg_keys[3], (HEADS, DH), jnp.float32) ** steps_of(arg_keys[3], (HEADS, DH), ((0, 16),), -0.2, 0.2)), 0.25, 2.5)
    reg = jnp.clip(jnp.exp(math.log(4.0) - 2.0794415 * jax.random.uniform(arg_keys[4], (HEADS,), jnp.float32) ** steps_of(arg_keys[4], (HEADS,), ((0, 16),), -0.2, 0.2)), 0.5, 4.0)
    norm_gain = jnp.clip(1.0 + 0.1 * jax.random.normal(arg_keys[5], (HEADS, DH), jnp.float32), 0.5, 1.5)
    out_weight = noise_with(arg_keys[6], (HEADS * DH, D), (HEADS * DH) ** -0.5, 0.1875, ((0, 16),), (0, 1, 16, 2.0))
    return {"queries": queries, "keys": keys, "values": values, "key_gain": key_gain, "reg": reg, "norm_gain": norm_gain, "out_weight": out_weight}


def solve_block(query_rows, key_rows, value_rows, key_state, value_state, lam):
    highest = lax.Precision.HIGHEST
    count = query_rows.shape[0]
    causal = jnp.tril(jnp.ones((count, count), jnp.float32))

    def apply_op(vec):
        scores = jnp.dot(vec, key_rows.T, precision=highest) * causal
        return jnp.dot(vec, key_state, precision=highest) + jnp.dot(scores, key_rows, precision=highest) + lam * vec
    guess = jnp.zeros_like(query_rows)
    resid = query_rows
    search = query_rows
    rr_now = lax.optimization_barrier(jnp.sum(resid * resid, axis=-1, keepdims=True))
    for step in range(ITERS):
        image = apply_op(search)
        active = rr_now > 1e-30
        curve = lax.optimization_barrier(jnp.sum(search * image, axis=-1, keepdims=True))
        alpha = jnp.where(active, rr_now / jnp.where(active, curve, 1.0), 0.0)
        guess = guess + alpha * search
        resid = resid - alpha * image
        rr_next = lax.optimization_barrier(jnp.sum(resid * resid, axis=-1, keepdims=True))
        ratio = jnp.where(active, rr_next / jnp.where(active, rr_now, 1.0), 0.0)
        search = resid + ratio * search
        rr_now = rr_next
    scores = jnp.dot(guess, key_rows.T, precision=highest) * causal
    return jnp.dot(guess, value_state, precision=highest) + jnp.dot(scores, value_rows, precision=highest)

def reference(queries, keys, values, key_gain, reg, norm_gain, out_weight):
    highest = lax.Precision.HIGHEST
    block = min(128, TOK_DEV)
    nblocks = TOKENS // block
    gained = (keys.astype(jnp.float32) * key_gain[None]).astype(jnp.bfloat16)

    def per_head(items):
        query_h, key_h, value_h, lam, gain_h = items
        qf = query_h.astype(jnp.float32).reshape(nblocks, block, DH)
        kf = key_h.astype(jnp.float32).reshape(nblocks, block, DH)
        vf = value_h.astype(jnp.float32).reshape(nblocks, block, DH)
        both = jnp.concatenate([kf, vf], axis=-1)
        grams = jnp.einsum('nbi,nbj->nij', kf, both, precision=highest)
        summed = jnp.cumsum(grams, axis=0)
        before = jnp.concatenate([jnp.zeros((1, DH, 2 * DH), jnp.float32), summed[:-1]], axis=0)
        read = jax.vmap(solve_block, in_axes=(0, 0, 0, 0, 0, None))(qf, kf, vf, before[:, :, :DH], before[:, :, DH:], lam)
        read = read.reshape(TOKENS, DH)
        square = lax.optimization_barrier(jnp.mean(read * read, axis=-1, keepdims=True))
        return (read * gain_h[None] * lax.rsqrt(square + 1e-06)).astype(jnp.bfloat16)
    normed = lax.map(per_head, (jnp.transpose(queries, (1, 0, 2)), jnp.transpose(gained, (1, 0, 2)), jnp.transpose(values, (1, 0, 2)), reg, norm_gain))
    laid = jnp.transpose(normed, (1, 0, 2)).reshape(TOKENS, HEADS * DH)
    return jnp.dot(laid, out_weight, preferred_element_type=jnp.float32).astype(jnp.bfloat16)
```

```python
import jax
import jax.numpy as jnp
from jax import lax
from jax.experimental import pallas as pl
from jax.experimental.pallas import tpu as pltpu
from jax.sharding import PartitionSpec as P

ITERS = 15
BLOCK = 128
F32 = jnp.float32
BF16 = jnp.bfloat16


def mm(a, b):
    return jnp.dot(a, b, preferred_element_type=F32)


def halves(value):
    high = value.astype(BF16)
    return high, (value - high.astype(F32)).astype(BF16)


def state_kernel(k_ref, v_ref, gain_ref, out_ref):
    gained = (k_ref[...].astype(F32) * gain_ref[...]).astype(BF16)
    width = gained.shape[1]
    over_tokens = (((0,), (0,)), ((), ()))
    out_ref[0:width, :] = lax.dot_general(
        gained, gained, over_tokens, preferred_element_type=F32
    )
    out_ref[width:, :] = lax.dot_general(
        v_ref[...], gained, over_tokens, preferred_element_type=F32
    )


def local_state(keys, values, gain):
    width = keys.shape[1]
    return pl.pallas_call(
        state_kernel,
        out_shape=jax.ShapeDtypeStruct((2 * width, width), F32),
        name="local_state",
    )(keys, values, gain)


def prefix_kernel(x_ref, o_ref):
    pieces, rows = o_ref.shape[0], o_ref.shape[1]
    total = jnp.zeros(o_ref.shape[1:], F32)
    for piece in range(pieces):
        o_ref[piece] = total
        total = total + x_ref[piece]


def exclusive(pieces):
    return pl.pallas_call(
        prefix_kernel,
        out_shape=jax.ShapeDtypeStruct(pieces.shape, F32),
        name="prefix",
    )(pieces)


def solve_kernel(
    reg_ref, q_ref, k_ref, v_ref, before_ref, gain_ref, norm_ref, out_ref,
    first, second, last, x_ref, r_ref, p_ref,
):
    width = q_ref.shape[1]
    blocks = q_ref.shape[0] // BLOCK
    lam = reg_ref[0]
    row = lax.broadcasted_iota(jnp.int32, (BLOCK, BLOCK), 0)
    col = lax.broadcasted_iota(jnp.int32, (BLOCK, BLOCK), 1)
    causal = row <= col
    h_state = before_ref[0:width, :]
    g_state = before_ref[width:, :]
    gain = gain_ref[...]
    starts = []
    for b in range(blocks):
        rows = pl.ds(b * BLOCK, BLOCK)
        key = (k_ref[rows, :].astype(F32) * gain).astype(BF16)
        key_t = key.astype(F32).T.astype(BF16)
        val_t = v_ref[rows, :].astype(F32).T.astype(BF16)
        high, low = halves(h_state)
        first[b, 0:width, 0:width] = high
        first[b, 0:width, width:] = high
        first[b, width:, 0:width] = key
        first[b, width:, width:] = key
        second[b, :, 0:BLOCK] = key_t
        second[b, :, BLOCK : 2 * BLOCK] = key_t
        second[b, :, 2 * BLOCK :] = low
        high, low = halves(g_state)
        last[b, :, 0:BLOCK] = val_t
        last[b, :, BLOCK : 2 * BLOCK] = val_t
        last[b, :, 2 * BLOCK : 3 * BLOCK] = low
        last[b, :, 3 * BLOCK : 4 * BLOCK] = high
        if b + 1 < blocks:
            h_state = h_state + mm(key_t, key)
            g_state = g_state + mm(val_t, key)
        query = q_ref[rows, :].astype(F32).T
        x_ref[b] = jnp.zeros_like(query)
        r_ref[b] = query
        p_ref[b] = query
        starts.append(jnp.sum(query * query, axis=0, keepdims=True))

    def step(_, rrs):
        news = []
        for b in range(blocks):
            p = p_ref[b]
            p_high, p_low = halves(p)
            one = mm(first[b], jnp.concatenate([p_high, p_low], axis=0))
            s_high, s_low = halves(jnp.where(causal, one[width:], 0.0))
            two = mm(second[b], jnp.concatenate([s_high, s_low, p_high], axis=0))
            w = one[:width] + two + lam * p
            rr = rrs[b]
            active = rr > 1e-30
            curve = jnp.sum(p * w, axis=0, keepdims=True)
            alpha = jnp.where(active, rr / jnp.where(active, curve, 1.0), 0.0)
            x_ref[b] = x_ref[b] + alpha * p
            r = r_ref[b] - alpha * w
            r_ref[b] = r
            new = jnp.sum(r * r, axis=0, keepdims=True)
            ratio = jnp.where(active, new / jnp.where(active, rr, 1.0), 0.0)
            p_ref[b] = r + ratio * p
            news.append(new)
        return tuple(news)

    lax.fori_loop(0, ITERS, step, tuple(starts))

    norm_col = jnp.broadcast_to(norm_ref[...], (BLOCK, width)).T
    for b in range(blocks):
        x_high, x_low = halves(x_ref[b])
        key = first[b, width:, :]
        scores = mm(key, jnp.concatenate([x_high, x_low], axis=0))
        s_high, s_low = halves(jnp.where(causal, scores, 0.0))
        read = mm(
            last[b],
            jnp.concatenate([s_high, s_low, x_high, x_high], axis=0),
        ) + mm(last[b, :, 3 * BLOCK :], x_low)
        square = jnp.mean(read * read, axis=0, keepdims=True)
        normed = read * norm_col * lax.rsqrt(square + 1e-06)
        out_ref[:, b * BLOCK : (b + 1) * BLOCK] = normed.astype(BF16)


def solve(reg, queries, keys, values, before, gain, norm_gain):
    tokens, width = queries.shape
    blocks = tokens // BLOCK
    vmem = pl.BlockSpec(memory_space=pltpu.VMEM)
    return pl.pallas_call(
        solve_kernel,
        out_shape=jax.ShapeDtypeStruct((width, tokens), BF16),
        in_specs=[pl.BlockSpec(memory_space=pltpu.SMEM)] + [vmem] * 6,
        out_specs=vmem,
        scratch_shapes=[
            pltpu.VMEM((blocks, 2 * BLOCK, 2 * width), BF16),
            pltpu.VMEM((blocks, width, 3 * BLOCK), BF16),
            pltpu.VMEM((blocks, width, 4 * BLOCK), BF16),
            pltpu.VMEM((blocks, width, BLOCK), F32),
            pltpu.VMEM((blocks, width, BLOCK), F32),
            pltpu.VMEM((blocks, width, BLOCK), F32),
        ],
        compiler_params=pltpu.CompilerParams(vmem_limit_bytes=40 * 2**20),
        name="solve",
    )(reg, queries, keys, values, before, gain, norm_gain)


def body(queries, keys, values, key_gain, reg, norm_gain, out_weight):
    width = keys.shape[2]
    devices = lax.axis_size("seq")
    key_rows, value_rows, query_rows = keys[:, 0, :], values[:, 0, :], queries[:, 0, :]
    state = local_state(key_rows, value_rows, key_gain)
    rows = 2 * width // devices
    parts = lax.all_to_all(
        state.reshape(devices, rows, width), "seq", 0, 0
    )
    earlier = exclusive(parts)
    before = lax.all_to_all(earlier, "seq", 0, 0)
    before = before.reshape(2 * width, width)
    normed = solve(reg, query_rows, key_rows, value_rows, before, key_gain, norm_gain)
    summed = lax.psum_scatter(
        lax.dot_general(
            out_weight, normed, (((0,), (0,)), ((), ())), preferred_element_type=F32
        ),
        "head",
        scatter_dimension=0,
        tiled=True,
    )
    return summed.T.astype(BF16)


def solution(mesh):
    return jax.shard_map(
        body,
        mesh=mesh,
        in_specs=(
            P("seq", "head", None),
            P("seq", "head", None),
            P("seq", "head", None),
            P("head", None),
            P("head"),
            P("head", None),
            P("head", None),
        ),
        out_specs=P("seq", "head"),
        check_vma=False,
    )
```

```python
import functools

import jax
import jax.numpy as jnp
from jax import lax
from jax.experimental import pallas as pl
from jax.experimental.pallas import tpu as pltpu
from jax.sharding import PartitionSpec as P

ITERS = 15
BLOCK = 128
F32 = jnp.float32
BF16 = jnp.bfloat16


def mm(a, b):
    return jnp.dot(a, b, preferred_element_type=F32)


def halves(value):
    high = value.astype(BF16)
    return high, (value - high.astype(F32)).astype(BF16)


def state_kernel(k_ref, v_ref, gain_ref, out_ref):
    gained = (k_ref[...].astype(F32) * gain_ref[...]).astype(BF16)
    width = gained.shape[1]
    over_tokens = (((0,), (0,)), ((), ()))
    out_ref[0:width, :] = lax.dot_general(
        gained, gained, over_tokens, preferred_element_type=F32
    )
    out_ref[width:, :] = lax.dot_general(
        v_ref[...], gained, over_tokens, preferred_element_type=F32
    )


def local_state(keys, values, gain):
    width = keys.shape[1]
    return pl.pallas_call(
        state_kernel,
        out_shape=jax.ShapeDtypeStruct((2 * width, width), F32),
        name="local_state",
    )(keys, values, gain)


def prefix_kernel(x_ref, o_ref):
    pieces, rows = o_ref.shape[0], o_ref.shape[1]
    total = jnp.zeros(o_ref.shape[1:], F32)
    for piece in range(pieces):
        o_ref[piece] = total
        total = total + x_ref[piece]


def exclusive(pieces):
    return pl.pallas_call(
        prefix_kernel,
        out_shape=jax.ShapeDtypeStruct(pieces.shape, F32),
        name="prefix",
    )(pieces)


def solve_kernel(
    reg_ref, q_ref, k_ref, v_ref, before_ref, gain_ref, norm_ref, out_ref,
    q_buf, k_buf, v_buf, first, second, last, x_ref, r_ref, p_ref, sems,
):
    copies = [
        pltpu.make_async_copy(source, target, sems.at[i])
        for i, (source, target) in enumerate(
            ((k_ref, k_buf), (v_ref, v_buf), (q_ref, q_buf))
        )
    ]
    for copy in copies:
        copy.start()
    for copy in copies:
        copy.wait()
    width = q_ref.shape[1]
    blocks = q_ref.shape[0] // BLOCK
    lam = reg_ref[0]
    row = lax.broadcasted_iota(jnp.int32, (BLOCK, BLOCK), 0)
    col = lax.broadcasted_iota(jnp.int32, (BLOCK, BLOCK), 1)
    causal = row <= col
    h_state = before_ref[0:width, :]
    g_state = before_ref[width:, :]
    gain = gain_ref[...]
    starts = []
    for b in range(blocks):
        rows = pl.ds(b * BLOCK, BLOCK)
        key = (k_buf[rows, :].astype(F32) * gain).astype(BF16)
        key_t = key.astype(F32).T.astype(BF16)
        val_t = v_buf[rows, :].astype(F32).T.astype(BF16)
        high, low = halves(h_state)
        first[b, 0:width, 0:width] = high
        first[b, 0:width, width:] = high
        first[b, width:, 0:width] = key
        first[b, width:, width:] = key
        second[b, :, 0:BLOCK] = key_t
        second[b, :, BLOCK : 2 * BLOCK] = key_t
        second[b, :, 2 * BLOCK :] = low
        high, low = halves(g_state)
        last[b, :, 0:BLOCK] = val_t
        last[b, :, BLOCK : 2 * BLOCK] = val_t
        last[b, :, 2 * BLOCK : 3 * BLOCK] = low
        last[b, :, 3 * BLOCK : 4 * BLOCK] = high
        if b + 1 < blocks:
            h_state = h_state + mm(key_t, key)
            g_state = g_state + mm(val_t, key)
        query = q_buf[rows, :].astype(F32).T
        x_ref[b] = jnp.zeros_like(query)
        r_ref[b] = query
        p_ref[b] = query
        starts.append(jnp.sum(query * query, axis=0, keepdims=True))

    def step(_, rrs):
        news = []
        for b in range(blocks):
            p = p_ref[b]
            p_high, p_low = halves(p)
            one = mm(first[b], jnp.concatenate([p_high, p_low], axis=0))
            s_high, s_low = halves(jnp.where(causal, one[width:], 0.0))
            two = mm(second[b], jnp.concatenate([s_high, s_low, p_high], axis=0))
            w = one[:width] + two + lam * p
            rr = rrs[b]
            active = rr > 1e-30
            curve = jnp.sum(p * w, axis=0, keepdims=True)
            alpha = jnp.where(active, rr / jnp.where(active, curve, 1.0), 0.0)
            x_ref[b] = x_ref[b] + alpha * p
            r = r_ref[b] - alpha * w
            r_ref[b] = r
            new = jnp.sum(r * r, axis=0, keepdims=True)
            ratio = jnp.where(active, new / jnp.where(active, rr, 1.0), 0.0)
            p_ref[b] = r + ratio * p
            news.append(new)
        return tuple(news)

    lax.fori_loop(0, ITERS, step, tuple(starts))

    norm_col = jnp.broadcast_to(norm_ref[...], (BLOCK, width)).T
    for b in range(blocks):
        x_high, x_low = halves(x_ref[b])
        key = first[b, width:, :]
        scores = mm(key, jnp.concatenate([x_high, x_low], axis=0))
        s_high, s_low = halves(jnp.where(causal, scores, 0.0))
        read = mm(
            last[b],
            jnp.concatenate([s_high, s_low, x_high, x_high], axis=0),
        ) + mm(last[b, :, 3 * BLOCK :], x_low)
        square = jnp.mean(read * read, axis=0, keepdims=True)
        normed = read * norm_col * lax.rsqrt(square + 1e-06)
        out_ref[b * BLOCK : (b + 1) * BLOCK, :] = normed.T.astype(BF16).astype(F32)


def solve(reg, queries, keys, values, before, gain, norm_gain):
    tokens, width = queries.shape
    blocks = tokens // BLOCK
    vmem = pl.BlockSpec(memory_space=pltpu.VMEM)
    return pl.pallas_call(
        solve_kernel,
        out_shape=jax.ShapeDtypeStruct((tokens, width), F32),
        in_specs=[pl.BlockSpec(memory_space=pltpu.SMEM)]
        + [pl.BlockSpec(memory_space=pl.ANY)] * 3
        + [vmem] * 3,
        out_specs=vmem,
        scratch_shapes=[
            pltpu.VMEM((tokens, width), BF16),
            pltpu.VMEM((tokens, width), BF16),
            pltpu.VMEM((tokens, width), BF16),
            pltpu.VMEM((blocks, 2 * BLOCK, 2 * width), BF16),
            pltpu.VMEM((blocks, width, 3 * BLOCK), BF16),
            pltpu.VMEM((blocks, width, 4 * BLOCK), BF16),
            pltpu.VMEM((blocks, width, BLOCK), F32),
            pltpu.VMEM((blocks, width, BLOCK), F32),
            pltpu.VMEM((blocks, width, BLOCK), F32),
            pltpu.SemaphoreType.DMA((3,)),
        ],
        cost_estimate=pl.CostEstimate(
            flops=60 * 10**9, bytes_accessed=2**21, transcendentals=0
        ),
        compiler_params=pltpu.CompilerParams(vmem_limit_bytes=40 * 2**20),
        name="solve",
    )(reg, queries, keys, values, before, gain, norm_gain)


def join_kernel(axis, a_ref, b_ref, out_ref):
    out_ref[...] = jnp.concatenate([a_ref[...], b_ref[...]], axis=axis).astype(BF16)


def joined(first, second, axis):
    shape = list(first.shape)
    shape[axis] *= 2
    return pl.pallas_call(
        functools.partial(join_kernel, axis),
        out_shape=jax.ShapeDtypeStruct(tuple(shape), BF16),
        compiler_params=pltpu.CompilerParams(vmem_limit_bytes=24 * 2**20),
        name="joined",
    )(first, second)


def sort_kernel(core_ref, w_ref, mine_ref, theirs_ref):
    chips, _, width = mine_ref.shape
    first_core = core_ref[0] == 0
    for chip in range(chips):
        zero = w_ref[:, 2 * chip * width : (2 * chip + 1) * width].astype(F32)
        one = w_ref[:, (2 * chip + 1) * width : (2 * chip + 2) * width].astype(F32)
        mine_ref[chip] = jnp.where(first_core, zero, one)
        theirs_ref[chip] = jnp.where(first_core, one, zero)


def sorted_weight(out_weight):
    width = out_weight.shape[0]
    chips = out_weight.shape[1] // (2 * width)
    core = lax.rem(lax.axis_index("head").astype(jnp.uint32), jnp.uint32(2))
    core = core.astype(jnp.int32).reshape(1)
    shape = jax.ShapeDtypeStruct((chips, width, width), F32)
    return pl.pallas_call(
        sort_kernel,
        out_shape=(shape, shape),
        in_specs=[
            pl.BlockSpec(memory_space=pltpu.SMEM),
            pl.BlockSpec(memory_space=pltpu.VMEM),
        ],
        name="sorted_weight",
    )(core, out_weight)


def swapped(value):
    heads = lax.axis_size("head")
    return lax.ppermute(value, "head", [(i, i ^ 1) for i in range(heads)])


def project(normed, weight_pair):
    tokens, width = normed.shape
    heads = lax.axis_size("head")
    place = lax.axis_index("head")
    chips = heads // 2
    chip = lax.div(place.astype(jnp.uint32), jnp.uint32(2))
    right = [(i, (i + 2) % heads) for i in range(heads)]
    left = [(i, (i - 2) % heads) for i in range(heads)]
    weights = joined(*weight_pair, 1)
    both = joined(normed, swapped(normed), 1)
    half = tokens // 2
    early, late = both[:half], both[half:]

    def part(rows, ahead):
        index = lax.rem(chip + jnp.uint32((ahead + chips) % chips), jnp.uint32(chips))
        columns = lax.dynamic_index_in_dim(weights, index, axis=0, keepdims=False)
        return jnp.dot(rows, columns, preferred_element_type=F32)

    far = chips // 2
    flows = {}
    for away in range(far, 0, -1):
        for sign, perm in ((1, right), (-1, left)):
            for name, rows in (("early", early), ("late", late)):
                key = (sign, name)
                if away == far and key not in ((1, "early"), (-1, "late")):
                    continue
                term = part(rows, sign * away)
                if key in flows:
                    term = flows[key] + term
                flows[key] = lax.ppermute(term, "head", perm)
    done = [
        part(rows, 0) + flows[(1, name)] + flows[(-1, name)]
        for name, rows in (("early", early), ("late", late))
    ]
    return jnp.concatenate(done, axis=0).astype(BF16)


def body(queries, keys, values, key_gain, reg, norm_gain, out_weight):
    width = keys.shape[2]
    devices = lax.axis_size("seq")
    key_rows, value_rows, query_rows = keys[:, 0, :], values[:, 0, :], queries[:, 0, :]
    state = local_state(key_rows, value_rows, key_gain)
    rows = 2 * width // devices
    parts = lax.all_to_all(
        state.reshape(devices, rows, width), "seq", 0, 0
    )
    earlier = exclusive(parts)
    earlier, out_weight = lax.optimization_barrier((earlier, out_weight))
    before = lax.all_to_all(earlier, "seq", 0, 0)
    mine, theirs = sorted_weight(out_weight)
    before, *weight_pair = lax.optimization_barrier((before, mine, swapped(theirs)))
    before = before.reshape(2 * width, width)
    normed = solve(reg, query_rows, key_rows, value_rows, before, key_gain, norm_gain)
    return project(normed, weight_pair)


def solution(mesh):
    return jax.shard_map(
        body,
        mesh=mesh,
        in_specs=(
            P("seq", "head", None),
            P("seq", "head", None),
            P("seq", "head", None),
            P("head", None),
            P("head"),
            P("head", None),
            P("head", None),
        ),
        out_specs=P("seq", "head"),
        check_vma=False,
    )
```

```python
import functools

import jax
import jax.numpy as jnp
from jax import lax
from jax.experimental import pallas as pl
from jax.experimental.pallas import tpu as pltpu
from jax.sharding import PartitionSpec as P

ITERS = 15
BLOCK = 128
F32 = jnp.float32
BF16 = jnp.bfloat16


def mm(a, b):
    return jnp.dot(a, b, preferred_element_type=F32)


def halves(value):
    high = value.astype(BF16)
    return high, (value - high.astype(F32)).astype(BF16)


def state_kernel(k_ref, v_ref, gain_ref, out_ref):
    gained = (k_ref[...].astype(F32) * gain_ref[...]).astype(BF16)
    width = gained.shape[1]
    over_tokens = (((0,), (0,)), ((), ()))
    out_ref[0:width, :] = lax.dot_general(
        gained, gained, over_tokens, preferred_element_type=F32
    )
    out_ref[width:, :] = lax.dot_general(
        v_ref[...], gained, over_tokens, preferred_element_type=F32
    )


def local_state(keys, values, gain):
    width = keys.shape[1]
    return pl.pallas_call(
        state_kernel,
        out_shape=jax.ShapeDtypeStruct((2 * width, width), F32),
        name="local_state",
    )(keys, values, gain)


def prefix_kernel(x_ref, o_ref):
    pieces, rows = o_ref.shape[0], o_ref.shape[1]
    total = jnp.zeros(o_ref.shape[1:], F32)
    for piece in range(pieces):
        o_ref[piece] = total
        total = total + x_ref[piece]


def exclusive(pieces):
    return pl.pallas_call(
        prefix_kernel,
        out_shape=jax.ShapeDtypeStruct(pieces.shape, F32),
        name="prefix",
    )(pieces)


def solve_kernel(
    reg_ref, q_ref, k_ref, v_ref, before_ref, gain_ref, norm_ref, out_ref,
    q_buf, k_buf, v_buf, first, second, last, x_ref, r_ref, p_ref, sems,
):
    copies = [
        pltpu.make_async_copy(source, target, sems.at[i])
        for i, (source, target) in enumerate(
            ((k_ref, k_buf), (v_ref, v_buf), (q_ref, q_buf))
        )
    ]
    for copy in copies:
        copy.start()
    for copy in copies:
        copy.wait()
    width = q_ref.shape[1]
    blocks = q_ref.shape[0] // BLOCK
    lam = reg_ref[0]
    row = lax.broadcasted_iota(jnp.int32, (BLOCK, BLOCK), 0)
    col = lax.broadcasted_iota(jnp.int32, (BLOCK, BLOCK), 1)
    causal = row <= col
    h_state = before_ref[0:width, :]
    g_state = before_ref[width:, :]
    gain = gain_ref[...]
    starts = []
    for b in range(blocks):
        rows = pl.ds(b * BLOCK, BLOCK)
        key = (k_buf[rows, :].astype(F32) * gain).astype(BF16)
        key_t = key.astype(F32).T.astype(BF16)
        val_t = v_buf[rows, :].astype(F32).T.astype(BF16)
        high, low = halves(h_state)
        first[b, 0:width, 0:width] = high
        first[b, 0:width, width:] = high
        first[b, width:, 0:width] = key
        first[b, width:, width:] = key
        second[b, :, 0:BLOCK] = key_t
        second[b, :, BLOCK : 2 * BLOCK] = key_t
        second[b, :, 2 * BLOCK :] = low
        high, low = halves(g_state)
        last[b, :, 0:BLOCK] = val_t
        last[b, :, BLOCK : 2 * BLOCK] = val_t
        last[b, :, 2 * BLOCK : 3 * BLOCK] = low
        last[b, :, 3 * BLOCK : 4 * BLOCK] = high
        if b + 1 < blocks:
            h_state = h_state + mm(key_t, key)
            g_state = g_state + mm(val_t, key)
        query = q_buf[rows, :].astype(F32).T
        x_ref[b] = jnp.zeros_like(query)
        r_ref[b] = query
        p_ref[b] = query
        starts.append(jnp.sum(query * query, axis=0, keepdims=True))

    def step(_, rrs):
        news = []
        for group in (range(blocks),):
            ps = {b: p_ref[b] for b in group}
            hs = {b: halves(ps[b]) for b in group}
            one = {
                b: mm(first[b], jnp.concatenate(hs[b], axis=0)) for b in group
            }
            ss = {b: halves(jnp.where(causal, one[b][width:], 0.0)) for b in group}
            two = {
                b: mm(second[b], jnp.concatenate([*ss[b], hs[b][0]], axis=0))
                for b in group
            }
            for b in group:
                p = p_ref[b]
                w = one[b][:width] + two[b] + lam * p
                rr = rrs[b]
                active = rr > 1e-30
                curve = jnp.sum(p * w, axis=0, keepdims=True)
                alpha = jnp.where(active, rr / jnp.where(active, curve, 1.0), 0.0)
                x_ref[b] = x_ref[b] + alpha * p
                r = r_ref[b] - alpha * w
                r_ref[b] = r
                new = jnp.sum(r * r, axis=0, keepdims=True)
                ratio = jnp.where(active, new / jnp.where(active, rr, 1.0), 0.0)
                p_ref[b] = r + ratio * p
                news.append(new)
        return tuple(news)

    lax.fori_loop(0, ITERS, step, tuple(starts))

    norm_col = jnp.broadcast_to(norm_ref[...], (BLOCK, width)).T
    for b in range(blocks):
        x_high, x_low = halves(x_ref[b])
        key = first[b, width:, :]
        scores = mm(key, jnp.concatenate([x_high, x_low], axis=0))
        s_high, s_low = halves(jnp.where(causal, scores, 0.0))
        read = mm(
            last[b],
            jnp.concatenate([s_high, s_low, x_high, x_high], axis=0),
        ) + mm(last[b, :, 3 * BLOCK :], x_low)
        square = jnp.mean(read * read, axis=0, keepdims=True)
        normed = read * norm_col * lax.rsqrt(square + 1e-06)
        out_ref[b * BLOCK : (b + 1) * BLOCK, :] = normed.T.astype(BF16).astype(F32)


def solve(reg, queries, keys, values, before, gain, norm_gain):
    tokens, width = queries.shape
    blocks = tokens // BLOCK
    vmem = pl.BlockSpec(memory_space=pltpu.VMEM)
    return pl.pallas_call(
        solve_kernel,
        out_shape=jax.ShapeDtypeStruct((tokens, width), F32),
        in_specs=[pl.BlockSpec(memory_space=pltpu.SMEM)]
        + [pl.BlockSpec(memory_space=pl.ANY)] * 3
        + [vmem] * 3,
        out_specs=vmem,
        scratch_shapes=[
            pltpu.VMEM((tokens, width), BF16),
            pltpu.VMEM((tokens, width), BF16),
            pltpu.VMEM((tokens, width), BF16),
            pltpu.VMEM((blocks, 2 * BLOCK, 2 * width), BF16),
            pltpu.VMEM((blocks, width, 3 * BLOCK), BF16),
            pltpu.VMEM((blocks, width, 4 * BLOCK), BF16),
            pltpu.VMEM((blocks, width, BLOCK), F32),
            pltpu.VMEM((blocks, width, BLOCK), F32),
            pltpu.VMEM((blocks, width, BLOCK), F32),
            pltpu.SemaphoreType.DMA((3,)),
        ],
        cost_estimate=pl.CostEstimate(
            flops=60 * 10**9, bytes_accessed=2**21, transcendentals=0
        ),
        compiler_params=pltpu.CompilerParams(vmem_limit_bytes=40 * 2**20),
        name="solve",
    )(reg, queries, keys, values, before, gain, norm_gain)


def swapped(value):
    heads = lax.axis_size("head")
    return lax.ppermute(value, "head", [(i, i ^ 1) for i in range(heads)])


def join_weight_kernel(own_ref, other_ref, out_ref):
    chips, double, columns = out_ref.shape
    half = double // 2
    for chip in range(chips):
        here = slice(chip * columns, (chip + 1) * columns)
        out_ref[chip, 0:half, :] = own_ref[:, here]
        out_ref[chip, half:, :] = other_ref[:, here].astype(BF16)


def join_weight(own, other):
    width, columns = own.shape
    return pl.pallas_call(
        join_weight_kernel,
        out_shape=jax.ShapeDtypeStruct((columns // (2 * width), 2 * width, 2 * width), BF16),
        name="join_weight",
    )(own, other)


def join_rows_kernel(own_ref, other_ref, out_ref):
    width = own_ref.shape[1]
    out_ref[:, 0:width] = own_ref[...].astype(BF16)
    out_ref[:, width:] = other_ref[...].astype(BF16)


def join_rows(own, other):
    tokens, width = own.shape
    return pl.pallas_call(
        join_rows_kernel,
        out_shape=jax.ShapeDtypeStruct((tokens, 2 * width), BF16),
        name="join_rows",
    )(own, other)


def project(normed, weights):
    tokens, width = normed.shape
    heads = lax.axis_size("head")
    place = lax.axis_index("head").astype(jnp.uint32)
    chips = heads // 2
    chip, core = lax.div(place, jnp.uint32(2)), lax.rem(place, jnp.uint32(2))
    left_going = core == 1
    ring = [(i, (i + (2 if i % 2 == 0 else heads - 2)) % heads) for i in range(heads)]
    both = join_rows(normed, swapped(normed))
    half = tokens // 2
    early, late = both[:half], both[half:]
    rows = (
        jnp.where(left_going, late, early),
        jnp.where(left_going, early, late),
    )

    def part(piece, away):
        ahead = jnp.where(left_going, jnp.uint32(chips - away), jnp.uint32(away % chips))
        index = lax.rem(chip + ahead, jnp.uint32(chips))
        columns = lax.dynamic_index_in_dim(weights, index, axis=0, keepdims=False)
        return jnp.dot(rows[piece], columns, preferred_element_type=F32)

    flows = [None, None]
    for away in range(chips // 2, 0, -1):
        for piece in (0, 1):
            if away == chips // 2 and piece == 1:
                continue
            term = part(piece, away)
            if flows[piece] is not None:
                term = flows[piece] + term
            flows[piece] = lax.ppermute(term, "head", ring)

    def columns_of(value, other):
        zero, one = value[:, :width], value[:, width:]
        return jnp.where(left_going != other, one, zero)

    given = [swapped(columns_of(flow, True)) for flow in flows]
    done = [
        columns_of(part(piece, 0) + flows[piece], False) + given[1 - piece]
        for piece in (0, 1)
    ]
    first, second = (value.astype(BF16) for value in done)
    return jnp.where(
        left_going,
        jnp.concatenate([second, first], axis=0),
        jnp.concatenate([first, second], axis=0),
    )


def body(queries, keys, values, key_gain, reg, norm_gain, out_weight):
    width = keys.shape[2]
    devices = lax.axis_size("seq")
    key_rows, value_rows, query_rows = keys[:, 0, :], values[:, 0, :], queries[:, 0, :]
    state = local_state(key_rows, value_rows, key_gain)
    rows = 2 * width // devices
    state, out_weight = lax.optimization_barrier((state, out_weight))
    parts = lax.all_to_all(state.reshape(devices, rows, width), "seq", 0, 0)
    weights = join_weight(out_weight, swapped(out_weight.astype(F32)))
    parts, weights = lax.optimization_barrier((parts, weights))
    before = lax.all_to_all(exclusive(parts), "seq", 0, 0)
    before = before.reshape(2 * width, width)
    normed = solve(reg, query_rows, key_rows, value_rows, before, key_gain, norm_gain)
    return project(normed, weights)


def solution(mesh):
    return jax.shard_map(
        body,
        mesh=mesh,
        in_specs=(
            P("seq", "head", None),
            P("seq", "head", None),
            P("seq", "head", None),
            P("head", None),
            P("head"),
            P("head", None),
            P("head", None),
        ),
        out_specs=P("seq", "head"),
        check_vma=False,
    )
```

```python
import functools

import jax
import jax.numpy as jnp
from jax import lax
from jax.experimental import pallas as pl
from jax.experimental.pallas import tpu as pltpu
from jax.sharding import PartitionSpec as P

ITERS = 15
BLOCK = 128
F32 = jnp.float32
BF16 = jnp.bfloat16


def mm(a, b):
    return jnp.dot(a, b, preferred_element_type=F32)


def halves(value):
    high = value.astype(BF16)
    return high, (value - high.astype(F32)).astype(BF16)


def state_kernel(k_ref, v_ref, gain_ref, out_ref):
    gained = (k_ref[...].astype(F32) * gain_ref[...]).astype(BF16)
    width = gained.shape[1]
    over_tokens = (((0,), (0,)), ((), ()))
    out_ref[0:width, :] = lax.dot_general(
        gained, gained, over_tokens, preferred_element_type=F32
    )
    out_ref[width:, :] = lax.dot_general(
        v_ref[...], gained, over_tokens, preferred_element_type=F32
    )


def local_state(keys, values, gain):
    width = keys.shape[1]
    return pl.pallas_call(
        state_kernel,
        out_shape=jax.ShapeDtypeStruct((2 * width, width), F32),
        name="local_state",
    )(keys, values, gain)


def prefix_kernel(x_ref, o_ref):
    pieces, rows = o_ref.shape[0], o_ref.shape[1]
    total = jnp.zeros(o_ref.shape[1:], F32)
    for piece in range(pieces):
        o_ref[piece] = total
        total = total + x_ref[piece]


def exclusive(pieces):
    return pl.pallas_call(
        prefix_kernel,
        out_shape=jax.ShapeDtypeStruct(pieces.shape, F32),
        name="prefix",
    )(pieces)


def solve_kernel(
    reg_ref, q_ref, k_ref, v_ref, before_ref, gain_ref, norm_ref, early_ref, late_ref,
    q_buf, k_buf, v_buf, first, second, last, x_ref, r_ref, p_ref, sems,
):
    copies = [
        pltpu.make_async_copy(source, target, sems.at[i])
        for i, (source, target) in enumerate(
            ((k_ref, k_buf), (v_ref, v_buf), (q_ref, q_buf))
        )
    ]
    for copy in copies:
        copy.start()
    for copy in copies:
        copy.wait()
    width = q_ref.shape[1]
    blocks = q_ref.shape[0] // BLOCK
    lam = reg_ref[0]
    row = lax.broadcasted_iota(jnp.int32, (BLOCK, BLOCK), 0)
    col = lax.broadcasted_iota(jnp.int32, (BLOCK, BLOCK), 1)
    causal = row <= col
    h_state = before_ref[0:width, :]
    g_state = before_ref[width:, :]
    gain = gain_ref[...]
    starts = []
    for b in range(blocks):
        rows = pl.ds(b * BLOCK, BLOCK)
        key = (k_buf[rows, :].astype(F32) * gain).astype(BF16)
        key_t = key.astype(F32).T.astype(BF16)
        val_t = v_buf[rows, :].astype(F32).T.astype(BF16)
        high, low = halves(h_state)
        first[b, 0:width, 0:width] = high
        first[b, 0:width, width:] = high
        first[b, width:, 0:width] = key
        first[b, width:, width:] = key
        second[b, :, 0:BLOCK] = key_t
        second[b, :, BLOCK : 2 * BLOCK] = key_t
        second[b, :, 2 * BLOCK :] = low
        high, low = halves(g_state)
        last[b, :, 0:BLOCK] = val_t
        last[b, :, BLOCK : 2 * BLOCK] = val_t
        last[b, :, 2 * BLOCK : 3 * BLOCK] = low
        last[b, :, 3 * BLOCK : 4 * BLOCK] = high
        if b + 1 < blocks:
            h_state = h_state + mm(key_t, key)
            g_state = g_state + mm(val_t, key)
        query = q_buf[rows, :].astype(F32).T
        x_ref[b] = jnp.zeros_like(query)
        r_ref[b] = query
        p_ref[b] = query
        starts.append(jnp.sum(query * query, axis=0, keepdims=True))

    def step(_, rrs):
        news = []
        for group in (range(blocks),):
            ps = {b: p_ref[b] for b in group}
            hs = {b: halves(ps[b]) for b in group}
            one = {
                b: mm(first[b], jnp.concatenate(hs[b], axis=0)) for b in group
            }
            ss = {b: halves(jnp.where(causal, one[b][width:], 0.0)) for b in group}
            two = {
                b: mm(second[b], jnp.concatenate([*ss[b], hs[b][0]], axis=0))
                for b in group
            }
            for b in group:
                p = p_ref[b]
                w = one[b][:width] + two[b] + lam * p
                rr = rrs[b]
                active = rr > 1e-30
                curve = jnp.sum(p * w, axis=0, keepdims=True)
                alpha = jnp.where(active, rr / jnp.where(active, curve, 1.0), 0.0)
                x_ref[b] = x_ref[b] + alpha * p
                r = r_ref[b] - alpha * w
                r_ref[b] = r
                new = jnp.sum(r * r, axis=0, keepdims=True)
                ratio = jnp.where(active, new / jnp.where(active, rr, 1.0), 0.0)
                p_ref[b] = r + ratio * p
                news.append(new)
        return tuple(news)

    lax.fori_loop(0, ITERS, step, tuple(starts))

    norm_col = jnp.broadcast_to(norm_ref[...], (BLOCK, width)).T
    for b in range(blocks):
        x_high, x_low = halves(x_ref[b])
        key = first[b, width:, :]
        scores = mm(key, jnp.concatenate([x_high, x_low], axis=0))
        s_high, s_low = halves(jnp.where(causal, scores, 0.0))
        read = mm(
            last[b],
            jnp.concatenate([s_high, s_low, x_high, x_high], axis=0),
        ) + mm(last[b, :, 3 * BLOCK :], x_low)
        square = jnp.mean(read * read, axis=0, keepdims=True)
        normed = read * norm_col * lax.rsqrt(square + 1e-06)
        out_ref = early_ref if 2 * b < blocks else late_ref
        place = (b % (blocks // 2)) * BLOCK
        out_ref[place : place + BLOCK, :] = normed.T.astype(BF16).astype(F32)


def solve(reg, queries, keys, values, before, gain, norm_gain):
    tokens, width = queries.shape
    blocks = tokens // BLOCK
    vmem = pl.BlockSpec(memory_space=pltpu.VMEM)
    return pl.pallas_call(
        solve_kernel,
        out_shape=(jax.ShapeDtypeStruct((tokens // 2, width), F32),) * 2,
        in_specs=[pl.BlockSpec(memory_space=pltpu.SMEM)]
        + [pl.BlockSpec(memory_space=pl.ANY)] * 3
        + [vmem] * 3,
        out_specs=(vmem, vmem),
        scratch_shapes=[
            pltpu.VMEM((tokens, width), BF16),
            pltpu.VMEM((tokens, width), BF16),
            pltpu.VMEM((tokens, width), BF16),
            pltpu.VMEM((blocks, 2 * BLOCK, 2 * width), BF16),
            pltpu.VMEM((blocks, width, 3 * BLOCK), BF16),
            pltpu.VMEM((blocks, width, 4 * BLOCK), BF16),
            pltpu.VMEM((blocks, width, BLOCK), F32),
            pltpu.VMEM((blocks, width, BLOCK), F32),
            pltpu.VMEM((blocks, width, BLOCK), F32),
            pltpu.SemaphoreType.DMA((3,)),
        ],
        cost_estimate=pl.CostEstimate(
            flops=60 * 10**9, bytes_accessed=2**21, transcendentals=0
        ),
        compiler_params=pltpu.CompilerParams(vmem_limit_bytes=40 * 2**20),
        name="solve",
    )(reg, queries, keys, values, before, gain, norm_gain)


def swapped(value):
    heads = lax.axis_size("head")
    return lax.ppermute(value, "head", [(i, i ^ 1) for i in range(heads)])


def join_weight_kernel(own_ref, other_ref, out_ref):
    chips, double, columns = out_ref.shape
    half = double // 2
    for chip in range(chips):
        here = slice(chip * columns, (chip + 1) * columns)
        out_ref[chip, 0:half, :] = own_ref[:, here]
        out_ref[chip, half:, :] = other_ref[:, here].astype(BF16)


def join_weight(own, other):
    width, columns = own.shape
    return pl.pallas_call(
        join_weight_kernel,
        out_shape=jax.ShapeDtypeStruct((columns // (2 * width), 2 * width, 2 * width), BF16),
        name="join_weight",
    )(own, other)


def open_kernel(where_ref, own_ref, other_ref, weights_ref, rows_ref, far_ref):
    width = own_ref.shape[1]
    rows = jnp.concatenate([own_ref[...], other_ref[...]], axis=1).astype(BF16)
    rows_ref[...] = rows
    columns = weights_ref[where_ref[0]]
    columns = jnp.where(where_ref[1] == 0, columns[:, :width], columns[:, width:])
    far_ref[...] = mm(rows, columns)


def opening(where, own, other, weights):
    tokens, width = own.shape
    vmem = pl.BlockSpec(memory_space=pltpu.VMEM)
    return pl.pallas_call(
        open_kernel,
        out_shape=(
            jax.ShapeDtypeStruct((tokens, 2 * width), BF16),
            jax.ShapeDtypeStruct((tokens, width), F32),
        ),
        in_specs=[pl.BlockSpec(memory_space=pltpu.SMEM), vmem, vmem, vmem],
        out_specs=(vmem, vmem),
        name="opening",
    )(where, own, other, weights)


def project(normed, weights):
    width = normed[0].shape[1]
    heads = lax.axis_size("head")
    place = lax.axis_index("head").astype(jnp.uint32)
    chips = heads // 2
    chip, core = lax.div(place, jnp.uint32(2)), lax.rem(place, jnp.uint32(2))
    left_going = core == 1
    step = lambda i: 2 if i % 2 == 0 else heads - 2
    ring = [(i, (i + step(i)) % heads) for i in range(heads)]
    cross = [(i, ((i + step(i)) % heads) ^ 1) for i in range(heads)]

    def index_of(away):
        ahead = jnp.where(left_going, jnp.uint32(chips - away), jnp.uint32(away % chips))
        return lax.rem(chip + ahead, jnp.uint32(chips))

    def part(rows, away):
        columns = lax.dynamic_index_in_dim(weights, index_of(away), axis=0, keepdims=False)
        return jnp.dot(rows, columns, preferred_element_type=F32)

    def own_columns(value):
        return jnp.where(left_going, value[:, width:], value[:, :width])

    def other_columns(value):
        return jnp.where(left_going, value[:, :width], value[:, width:])

    where = jnp.stack([index_of(chips // 2), core]).astype(jnp.int32)
    others = [swapped(half) for half in normed]
    halves_of, flows = [], []
    for own, other in zip(normed, others):
        rows, far = opening(where, own, other, weights)
        halves_of.append(rows)
        flows.append(lax.ppermute(far, "head", ring))
    for away in range(chips // 2 - 1, 1, -1):
        for piece, rows in enumerate(halves_of):
            flow = flows[piece]
            if flow.shape[1] == width:
                blank = jnp.zeros_like(flow)
                flow = jnp.concatenate(
                    [
                        jnp.where(left_going, blank, flow),
                        jnp.where(left_going, flow, blank),
                    ],
                    axis=1,
                )
            flows[piece] = lax.ppermute(flow + part(rows, away), "head", ring)
    done = []
    for piece, rows in enumerate(halves_of):
        last = flows[piece] + part(rows, 1)
        same = lax.ppermute(own_columns(last), "head", ring)
        crossed = lax.ppermute(other_columns(last), "head", cross)
        done.append((own_columns(part(rows, 0)) + same + crossed).astype(BF16))
    return jnp.concatenate(done, axis=0)


def body(queries, keys, values, key_gain, reg, norm_gain, out_weight):
    width = keys.shape[2]
    devices = lax.axis_size("seq")
    key_rows, value_rows, query_rows = keys[:, 0, :], values[:, 0, :], queries[:, 0, :]
    state = local_state(key_rows, value_rows, key_gain)
    rows = 2 * width // devices
    state, out_weight = lax.optimization_barrier((state, out_weight))
    parts = lax.all_to_all(state.reshape(devices, rows, width), "seq", 0, 0)
    weights = join_weight(out_weight, swapped(out_weight.astype(F32)))
    parts, weights = lax.optimization_barrier((parts, weights))
    before = lax.all_to_all(exclusive(parts), "seq", 0, 0)
    before = before.reshape(2 * width, width)
    normed = solve(reg, query_rows, key_rows, value_rows, before, key_gain, norm_gain)
    return project(normed, weights)


def solution(mesh):
    return jax.shard_map(
        body,
        mesh=mesh,
        in_specs=(
            P("seq", "head", None),
            P("seq", "head", None),
            P("seq", "head", None),
            P("head", None),
            P("head"),
            P("head", None),
            P("head", None),
        ),
        out_specs=P("seq", "head"),
        check_vma=False,
    )
```

```python
import functools

import jax
import jax.numpy as jnp
from jax import lax
from jax.experimental import pallas as pl
from jax.experimental.pallas import tpu as pltpu
from jax.sharding import PartitionSpec as P

ITERS = 15
BLOCK = 128
F32 = jnp.float32
BF16 = jnp.bfloat16


def mm(a, b):
    return jnp.dot(a, b, preferred_element_type=F32)


def halves(value):
    high = value.astype(BF16)
    return high, (value - high.astype(F32)).astype(BF16)


def small(mebibytes):
    return pltpu.CompilerParams(vmem_limit_bytes=mebibytes * 2**20)


def state_kernel(k_ref, v_ref, gain_ref, norm_ref, state_ref, gained_ref, column_ref):
    gained = (k_ref[...].astype(F32) * gain_ref[...]).astype(BF16)
    width = gained.shape[1]
    gained_ref[...] = gained
    over_tokens = (((0,), (0,)), ((), ()))
    state_ref[0:width, :] = lax.dot_general(
        gained, gained, over_tokens, preferred_element_type=F32
    )
    state_ref[width:, :] = lax.dot_general(
        v_ref[...], gained, over_tokens, preferred_element_type=F32
    )
    column_ref[...] = jnp.broadcast_to(norm_ref[...], column_ref.shape).T


def local_state(keys, values, gain, norm_gain):
    width = keys.shape[1]
    return pl.pallas_call(
        state_kernel,
        out_shape=(
            jax.ShapeDtypeStruct((2 * width, width), F32),
            jax.ShapeDtypeStruct(keys.shape, BF16),
            jax.ShapeDtypeStruct((width, width), F32),
        ),
        compiler_params=small(6),
        name="local_state",
    )(keys, values, gain, norm_gain)


def prefix_kernel(x_ref, o_ref):
    pieces, rows = o_ref.shape[0], o_ref.shape[1]
    total = jnp.zeros(o_ref.shape[1:], F32)
    for piece in range(pieces):
        o_ref[piece] = total
        total = total + x_ref[piece]


def exclusive(pieces):
    return pl.pallas_call(
        prefix_kernel,
        out_shape=jax.ShapeDtypeStruct(pieces.shape, F32),
        compiler_params=small(2),
        name="prefix",
    )(pieces)


def solve_kernel(
    reg_ref, q_ref, k_ref, v_ref, before_ref, column_ref, early_ref, late_ref,
    first, second, last, x_ref, r_ref, p_ref,
):
    width = q_ref.shape[1]
    blocks = q_ref.shape[0] // BLOCK
    lam = reg_ref[0]
    row = lax.broadcasted_iota(jnp.int32, (BLOCK, BLOCK), 0)
    col = lax.broadcasted_iota(jnp.int32, (BLOCK, BLOCK), 1)
    causal = row <= col
    h_state = before_ref[0:width, :]
    g_state = before_ref[width:, :]
    starts = []
    for b in range(blocks):
        rows = pl.ds(b * BLOCK, BLOCK)
        key = k_ref[rows, :]
        key_t = key.astype(F32).T.astype(BF16)
        val_t = v_ref[rows, :].astype(F32).T.astype(BF16)
        high, low = halves(h_state)
        first[b, 0:width, 0:width] = high
        first[b, 0:width, width:] = high
        first[b, width:, 0:width] = key
        first[b, width:, width:] = key
        second[b, :, 0:BLOCK] = key_t
        second[b, :, BLOCK : 2 * BLOCK] = key_t
        second[b, :, 2 * BLOCK :] = low
        high, low = halves(g_state)
        last[b, :, 0:BLOCK] = val_t
        last[b, :, BLOCK : 2 * BLOCK] = val_t
        last[b, :, 2 * BLOCK : 3 * BLOCK] = low
        last[b, :, 3 * BLOCK : 4 * BLOCK] = high
        if b + 1 < blocks:
            h_state = h_state + mm(key_t, key)
            g_state = g_state + mm(val_t, key)
        query = q_ref[rows, :].astype(F32).T
        x_ref[b] = jnp.zeros_like(query)
        r_ref[b] = query
        p_ref[b] = query
        starts.append(jnp.sum(query * query, axis=0, keepdims=True))

    def step(_, rrs):
        news = []
        for group in (range(blocks),):
            ps = {b: p_ref[b] for b in group}
            hs = {b: halves(ps[b]) for b in group}
            one = {
                b: mm(first[b], jnp.concatenate(hs[b], axis=0)) for b in group
            }
            ss = {b: halves(jnp.where(causal, one[b][width:], 0.0)) for b in group}
            two = {
                b: mm(second[b], jnp.concatenate([*ss[b], hs[b][0]], axis=0))
                for b in group
            }
            for b in group:
                p = p_ref[b]
                w = one[b][:width] + two[b] + lam * p
                rr = rrs[b]
                active = rr > 1e-30
                curve = jnp.sum(p * w, axis=0, keepdims=True)
                alpha = jnp.where(active, rr / jnp.where(active, curve, 1.0), 0.0)
                x_ref[b] = x_ref[b] + alpha * p
                r = r_ref[b] - alpha * w
                r_ref[b] = r
                new = jnp.sum(r * r, axis=0, keepdims=True)
                ratio = jnp.where(active, new / jnp.where(active, rr, 1.0), 0.0)
                p_ref[b] = r + ratio * p
                news.append(new)
        return tuple(news)

    lax.fori_loop(0, ITERS, step, tuple(starts))

    column = column_ref[...]
    for b in range(blocks):
        x_high, x_low = halves(x_ref[b])
        key = first[b, width:, :]
        scores = mm(key, jnp.concatenate([x_high, x_low], axis=0))
        s_high, s_low = halves(jnp.where(causal, scores, 0.0))
        read = mm(
            last[b],
            jnp.concatenate([s_high, s_low, x_high, x_high], axis=0),
        ) + mm(last[b, :, 3 * BLOCK :], x_low)
        square = jnp.mean(read * read, axis=0, keepdims=True)
        normed = read * column * lax.rsqrt(square + 1e-06)
        out_ref = early_ref if 2 * b < blocks else late_ref
        place = (b % (blocks // 2)) * BLOCK
        out_ref[place : place + BLOCK, :] = normed.T.astype(BF16).astype(F32)


def solve(reg, queries, keys, values, before, column):
    tokens, width = queries.shape
    blocks = tokens // BLOCK
    vmem = pl.BlockSpec(memory_space=pltpu.VMEM)
    return pl.pallas_call(
        solve_kernel,
        out_shape=(jax.ShapeDtypeStruct((tokens // 2, width), F32),) * 2,
        in_specs=[pl.BlockSpec(memory_space=pltpu.SMEM)] + [vmem] * 5,
        out_specs=(vmem, vmem),
        scratch_shapes=[
            pltpu.VMEM((blocks, 2 * BLOCK, 2 * width), BF16),
            pltpu.VMEM((blocks, width, 3 * BLOCK), BF16),
            pltpu.VMEM((blocks, width, 4 * BLOCK), BF16),
            pltpu.VMEM((blocks, width, BLOCK), F32),
            pltpu.VMEM((blocks, width, BLOCK), F32),
            pltpu.VMEM((blocks, width, BLOCK), F32),
        ],
        cost_estimate=pl.CostEstimate(
            flops=60 * 10**9, bytes_accessed=2**21, transcendentals=0
        ),
        compiler_params=pltpu.CompilerParams(vmem_limit_bytes=20 * 2**20),
        name="solve",
    )(reg, queries, keys, values, before, column)


def swapped(value):
    heads = lax.axis_size("head")
    return lax.ppermute(value, "head", [(i, i ^ 1) for i in range(heads)])


def join_weight_kernel(own_ref, other_ref, out_ref):
    chips, double, columns = out_ref.shape
    half = double // 2
    for chip in range(chips):
        here = slice(chip * columns, (chip + 1) * columns)
        out_ref[chip, 0:half, :] = own_ref[:, here]
        out_ref[chip, half:, :] = other_ref[:, here].astype(BF16)


def join_weight(own, other):
    width, columns = own.shape
    return pl.pallas_call(
        join_weight_kernel,
        out_shape=jax.ShapeDtypeStruct((columns // (2 * width), 2 * width, 2 * width), BF16),
        compiler_params=small(8),
        name="join_weight",
    )(own, other)


def open_kernel(where_ref, own_ref, other_ref, weights_ref, rows_ref, far_ref):
    width = own_ref.shape[1]
    rows = jnp.concatenate([own_ref[...], other_ref[...]], axis=1).astype(BF16)
    rows_ref[...] = rows
    columns = weights_ref[where_ref[0]]
    columns = jnp.where(where_ref[1] == 0, columns[:, :width], columns[:, width:])
    far_ref[...] = mm(rows, columns)


def opposite():
    place, heads = lax.axis_index("head").astype(jnp.uint32), lax.axis_size("head")
    chip, core = lax.div(place, jnp.uint32(2)), lax.rem(place, jnp.uint32(2))
    far = lax.rem(chip + jnp.uint32(heads // 4), jnp.uint32(heads // 2))
    return jnp.stack([far, core]).astype(jnp.int32)


def opening(where, own, other, weights):
    tokens, width = own.shape
    vmem = pl.BlockSpec(memory_space=pltpu.VMEM)
    return pl.pallas_call(
        open_kernel,
        out_shape=(
            jax.ShapeDtypeStruct((tokens, 2 * width), BF16),
            jax.ShapeDtypeStruct((tokens, width), F32),
        ),
        in_specs=[pl.BlockSpec(memory_space=pltpu.SMEM), vmem, vmem, vmem],
        out_specs=(vmem, vmem),
        compiler_params=small(8),
        name="opening",
    )(where, own, other, weights)


def project(normed, weights, where):
    width = normed[0].shape[1]
    heads = lax.axis_size("head")
    place = lax.axis_index("head").astype(jnp.uint32)
    chips = heads // 2
    chip, core = lax.div(place, jnp.uint32(2)), lax.rem(place, jnp.uint32(2))
    left_going = core == 1
    step = lambda i: 2 if i % 2 == 0 else heads - 2
    ring = [(i, (i + step(i)) % heads) for i in range(heads)]
    cross = [(i, ((i + step(i)) % heads) ^ 1) for i in range(heads)]

    def index_of(away):
        ahead = jnp.where(left_going, jnp.uint32(chips - away), jnp.uint32(away % chips))
        return lax.rem(chip + ahead, jnp.uint32(chips))

    def part(rows, away):
        columns = lax.dynamic_index_in_dim(weights, index_of(away), axis=0, keepdims=False)
        return jnp.dot(rows, columns, preferred_element_type=F32)

    def own_columns(value):
        return jnp.where(left_going, value[:, width:], value[:, :width])

    def other_columns(value):
        return jnp.where(left_going, value[:, :width], value[:, width:])

    others = [swapped(half) for half in normed]
    halves_of, flows = [], []
    for own, other in zip(normed, others):
        rows, far = opening(where, own, other, weights)
        halves_of.append(rows)
        flows.append(lax.ppermute(far, "head", ring))
    for away in range(chips // 2 - 1, 1, -1):
        for piece, rows in enumerate(halves_of):
            flow = flows[piece]
            if flow.shape[1] == width:
                blank = jnp.zeros_like(flow)
                flow = jnp.concatenate(
                    [
                        jnp.where(left_going, blank, flow),
                        jnp.where(left_going, flow, blank),
                    ],
                    axis=1,
                )
            flows[piece] = lax.ppermute(flow + part(rows, away), "head", ring)
    done = []
    for piece, rows in enumerate(halves_of):
        last = flows[piece] + part(rows, 1)
        same = lax.ppermute(own_columns(last), "head", ring)
        crossed = lax.ppermute(other_columns(last), "head", cross)
        done.append((own_columns(part(rows, 0)) + same + crossed).astype(BF16))
    return jnp.concatenate(done, axis=0)


def body(queries, keys, values, key_gain, reg, norm_gain, out_weight):
    width = keys.shape[2]
    devices = lax.axis_size("seq")
    key_rows, value_rows, query_rows = keys[:, 0, :], values[:, 0, :], queries[:, 0, :]
    state, gained, column = local_state(key_rows, value_rows, key_gain, norm_gain)
    rows = 2 * width // devices
    state, out_weight = lax.optimization_barrier((state, out_weight))
    parts = lax.all_to_all(state.reshape(devices, rows, width), "seq", 0, 0)
    weights = join_weight(out_weight, swapped(out_weight.astype(F32)))
    parts, weights, where = lax.optimization_barrier((parts, weights, opposite()))
    before = lax.all_to_all(exclusive(parts), "seq", 0, 0)
    before = before.reshape(2 * width, width)
    normed = solve(reg, query_rows, gained, value_rows, before, column)
    return project(normed, weights, where)


def solution(mesh):
    return jax.shard_map(
        body,
        mesh=mesh,
        in_specs=(
            P("seq", "head", None),
            P("seq", "head", None),
            P("seq", "head", None),
            P("head", None),
            P("head"),
            P("head", None),
            P("head", None),
        ),
        out_specs=P("seq", "head"),
        check_vma=False,
    )
```

```python
import functools

import jax
import jax.numpy as jnp
from jax import lax
from jax.experimental import pallas as pl
from jax.experimental.pallas import tpu as pltpu
from jax.sharding import PartitionSpec as P

ITERS = 15
BLOCK = 128
F32 = jnp.float32
BF16 = jnp.bfloat16


def mm(a, b):
    return jnp.dot(a, b, preferred_element_type=F32)


def halves(value):
    high = value.astype(BF16)
    return high, (value - high.astype(F32)).astype(BF16)


def small(mebibytes):
    return pltpu.CompilerParams(vmem_limit_bytes=mebibytes * 2**20)


def state_kernel(k_ref, v_ref, gain_ref, norm_ref, state_ref, gained_ref, column_ref):
    gained = (k_ref[...].astype(F32) * gain_ref[...]).astype(BF16)
    width = gained.shape[1]
    gained_ref[...] = gained
    over_tokens = (((0,), (0,)), ((), ()))
    state_ref[0:width, :] = lax.dot_general(
        gained, gained, over_tokens, preferred_element_type=F32
    )
    state_ref[width:, :] = lax.dot_general(
        v_ref[...], gained, over_tokens, preferred_element_type=F32
    )
    column_ref[...] = jnp.broadcast_to(norm_ref[...], column_ref.shape).T


def local_state(keys, values, gain, norm_gain):
    width = keys.shape[1]
    return pl.pallas_call(
        state_kernel,
        out_shape=(
            jax.ShapeDtypeStruct((2 * width, width), F32),
            jax.ShapeDtypeStruct(keys.shape, BF16),
            jax.ShapeDtypeStruct((width, width), F32),
        ),
        name="local_state",
    )(keys, values, gain, norm_gain)


def prefix_kernel(x_ref, o_ref):
    pieces, rows = o_ref.shape[0], o_ref.shape[1]
    total = jnp.zeros(o_ref.shape[1:], F32)
    for piece in range(pieces):
        o_ref[piece] = total
        total = total + x_ref[piece]


def exclusive(pieces):
    return pl.pallas_call(
        prefix_kernel,
        out_shape=jax.ShapeDtypeStruct(pieces.shape, F32),
        compiler_params=small(2),
        name="prefix",
    )(pieces)


def solve_kernel(
    reg_ref, q_ref, k_ref, v_ref, before_ref, column_ref, early_ref, late_ref,
    first, second, last, x_ref, r_ref, p_ref,
):
    width = q_ref.shape[1]
    blocks = q_ref.shape[0] // BLOCK
    lam = reg_ref[0]
    row = lax.broadcasted_iota(jnp.int32, (BLOCK, BLOCK), 0)
    col = lax.broadcasted_iota(jnp.int32, (BLOCK, BLOCK), 1)
    causal = row <= col
    h_state = before_ref[0:width, :]
    g_state = before_ref[width:, :]
    starts = []
    for b in range(blocks):
        rows = pl.ds(b * BLOCK, BLOCK)
        key = k_ref[rows, :]
        key_t = key.astype(F32).T.astype(BF16)
        val_t = v_ref[rows, :].astype(F32).T.astype(BF16)
        high, low = halves(h_state)
        first[b, 0:width, 0:width] = high
        first[b, 0:width, width:] = high
        first[b, width:, 0:width] = key
        first[b, width:, width:] = key
        second[b, :, 0:BLOCK] = key_t
        second[b, :, BLOCK : 2 * BLOCK] = key_t
        second[b, :, 2 * BLOCK :] = low
        high, low = halves(g_state)
        last[b, :, 0:BLOCK] = val_t
        last[b, :, BLOCK : 2 * BLOCK] = val_t
        last[b, :, 2 * BLOCK : 3 * BLOCK] = low
        last[b, :, 3 * BLOCK : 4 * BLOCK] = high
        if b + 1 < blocks:
            h_state = h_state + mm(key_t, key)
            g_state = g_state + mm(val_t, key)
        query = q_ref[rows, :].astype(F32).T
        x_ref[b] = jnp.zeros_like(query)
        r_ref[b] = query
        p_ref[b] = query
        starts.append(jnp.sum(query * query, axis=0, keepdims=True))

    def step(_, rrs):
        news = []
        for group in (range(blocks),):
            ps = {b: p_ref[b] for b in group}
            hs = {b: halves(ps[b]) for b in group}
            one = {
                b: mm(first[b], jnp.concatenate(hs[b], axis=0)) for b in group
            }
            ss = {b: halves(jnp.where(causal, one[b][width:], 0.0)) for b in group}
            two = {
                b: mm(second[b], jnp.concatenate([*ss[b], hs[b][0]], axis=0))
                for b in group
            }
            for b in group:
                p = p_ref[b]
                w = one[b][:width] + two[b] + lam * p
                rr = rrs[b]
                active = rr > 1e-30
                curve = jnp.sum(p * w, axis=0, keepdims=True)
                alpha = jnp.where(active, rr / jnp.where(active, curve, 1.0), 0.0)
                x_ref[b] = x_ref[b] + alpha * p
                r = r_ref[b] - alpha * w
                r_ref[b] = r
                new = jnp.sum(r * r, axis=0, keepdims=True)
                ratio = jnp.where(active, new / jnp.where(active, rr, 1.0), 0.0)
                p_ref[b] = r + ratio * p
                news.append(new)
        return tuple(news)

    lax.fori_loop(0, ITERS, step, tuple(starts))

    column = column_ref[...]
    for b in range(blocks):
        x_high, x_low = halves(x_ref[b])
        key = first[b, width:, :]
        scores = mm(key, jnp.concatenate([x_high, x_low], axis=0))
        s_high, s_low = halves(jnp.where(causal, scores, 0.0))
        read = mm(
            last[b],
            jnp.concatenate([s_high, s_low, x_high, x_high], axis=0),
        ) + mm(last[b, :, 3 * BLOCK :], x_low)
        square = jnp.mean(read * read, axis=0, keepdims=True)
        normed = read * column * lax.rsqrt(square + 1e-06)
        out_ref = early_ref if 2 * b < blocks else late_ref
        place = (b % (blocks // 2)) * BLOCK
        out_ref[place : place + BLOCK, :] = normed.T.astype(BF16).astype(F32)


def solve(reg, queries, keys, values, before, column):
    tokens, width = queries.shape
    blocks = tokens // BLOCK
    vmem = pl.BlockSpec(memory_space=pltpu.VMEM)
    return pl.pallas_call(
        solve_kernel,
        out_shape=(jax.ShapeDtypeStruct((tokens // 2, width), F32),) * 2,
        in_specs=[pl.BlockSpec(memory_space=pltpu.SMEM)] + [vmem] * 5,
        out_specs=(vmem, vmem),
        scratch_shapes=[
            pltpu.VMEM((blocks, 2 * BLOCK, 2 * width), BF16),
            pltpu.VMEM((blocks, width, 3 * BLOCK), BF16),
            pltpu.VMEM((blocks, width, 4 * BLOCK), BF16),
            pltpu.VMEM((blocks, width, BLOCK), F32),
            pltpu.VMEM((blocks, width, BLOCK), F32),
            pltpu.VMEM((blocks, width, BLOCK), F32),
        ],
        cost_estimate=pl.CostEstimate(
            flops=60 * 10**9, bytes_accessed=2**21, transcendentals=0
        ),
        compiler_params=pltpu.CompilerParams(vmem_limit_bytes=20 * 2**20),
        name="solve",
    )(reg, queries, keys, values, before, column)


def swapped(value):
    heads = lax.axis_size("head")
    return lax.ppermute(value, "head", [(i, i ^ 1) for i in range(heads)])


def join_weight_kernel(own_ref, other_ref, out_ref):
    chips, double, columns = out_ref.shape
    half = double // 2
    for chip in range(chips):
        here = slice(chip * columns, (chip + 1) * columns)
        out_ref[chip, 0:half, :] = own_ref[:, here]
        out_ref[chip, half:, :] = other_ref[:, here].astype(BF16)


def join_weight(own, other):
    width, columns = own.shape
    return pl.pallas_call(
        join_weight_kernel,
        out_shape=jax.ShapeDtypeStruct((columns // (2 * width), 2 * width, 2 * width), BF16),
        compiler_params=small(8),
        name="join_weight",
    )(own, other)


def open_kernel(where_ref, own_ref, other_ref, weights_ref, rows_ref, far_ref):
    width = own_ref.shape[1]
    rows = jnp.concatenate([own_ref[...], other_ref[...]], axis=1).astype(BF16)
    rows_ref[...] = rows
    columns = weights_ref[where_ref[0]]
    columns = jnp.where(where_ref[1] == 0, columns[:, :width], columns[:, width:])
    far_ref[...] = mm(rows, columns)


def opposite():
    place, heads = lax.axis_index("head").astype(jnp.uint32), lax.axis_size("head")
    chip, core = lax.div(place, jnp.uint32(2)), lax.rem(place, jnp.uint32(2))
    far = lax.rem(chip + jnp.uint32(heads // 4), jnp.uint32(heads // 2))
    return jnp.stack([far, core]).astype(jnp.int32)


def opening(where, own, other, weights):
    tokens, width = own.shape
    vmem = pl.BlockSpec(memory_space=pltpu.VMEM)
    return pl.pallas_call(
        open_kernel,
        out_shape=(
            jax.ShapeDtypeStruct((tokens, 2 * width), BF16),
            jax.ShapeDtypeStruct((tokens, width), F32),
        ),
        in_specs=[pl.BlockSpec(memory_space=pltpu.SMEM), vmem, vmem, vmem],
        out_specs=(vmem, vmem),
        compiler_params=small(8),
        name="opening",
    )(where, own, other, weights)


def project(normed, weights, where):
    width = normed[0].shape[1]
    heads = lax.axis_size("head")
    place = lax.axis_index("head").astype(jnp.uint32)
    chips = heads // 2
    chip, core = lax.div(place, jnp.uint32(2)), lax.rem(place, jnp.uint32(2))
    others = [swapped(half) for half in normed]
    rings, crosses, leftward, halves_of, flows = [], [], [], [], []
    for piece, (own, other) in enumerate(zip(normed, others)):
        step = [2 if (i + piece) % 2 == 0 else heads - 2 for i in range(heads)]
        rings.append([(i, (i + step[i]) % heads) for i in range(heads)])
        crosses.append([(i, ((i + step[i]) % heads) ^ 1) for i in range(heads)])
        leftward.append(core != piece)
        rows, far = opening(where, own, other, weights)
        halves_of.append(rows)
        flows.append(lax.ppermute(far, "head", rings[piece]))

    def part(piece, away):
        ahead = jnp.where(
            leftward[piece], jnp.uint32(chips - away), jnp.uint32(away % chips)
        )
        index = lax.rem(chip + ahead, jnp.uint32(chips))
        columns = lax.dynamic_index_in_dim(weights, index, axis=0, keepdims=False)
        return jnp.dot(halves_of[piece], columns, preferred_element_type=F32)

    def own_columns(value):
        return jnp.where(core == 1, value[:, width:], value[:, :width])

    def other_columns(value):
        return jnp.where(core == 1, value[:, :width], value[:, width:])

    for away in range(chips // 2 - 1, 1, -1):
        for piece, flow in enumerate(flows):
            if flow.shape[1] == width:
                blank = jnp.zeros_like(flow)
                flow = jnp.concatenate(
                    [
                        jnp.where(core == 1, blank, flow),
                        jnp.where(core == 1, flow, blank),
                    ],
                    axis=1,
                )
            flows[piece] = lax.ppermute(
                flow + part(piece, away), "head", rings[piece]
            )
    done = []
    for piece, flow in enumerate(flows):
        last = flow + part(piece, 1)
        same = lax.ppermute(own_columns(last), "head", rings[piece])
        crossed = lax.ppermute(other_columns(last), "head", crosses[piece])
        done.append((own_columns(part(piece, 0)) + same + crossed).astype(BF16))
    return jnp.concatenate(done, axis=0)


def body(queries, keys, values, key_gain, reg, norm_gain, out_weight):
    width = keys.shape[2]
    devices = lax.axis_size("seq")
    key_rows, value_rows, query_rows = keys[:, 0, :], values[:, 0, :], queries[:, 0, :]
    state, gained, column = local_state(key_rows, value_rows, key_gain, norm_gain)
    rows = 2 * width // devices
    state, out_weight = lax.optimization_barrier((state, out_weight))
    parts = lax.all_to_all(state.reshape(devices, rows, width), "seq", 0, 0)
    weights = join_weight(out_weight, swapped(out_weight.astype(F32)))
    parts, weights, where = lax.optimization_barrier((parts, weights, opposite()))
    before = lax.all_to_all(exclusive(parts), "seq", 0, 0)
    before = before.reshape(2 * width, width)
    normed = solve(reg, query_rows, gained, value_rows, before, column)
    return project(normed, weights, where)


def solution(mesh):
    return jax.shard_map(
        body,
        mesh=mesh,
        in_specs=(
            P("seq", "head", None),
            P("seq", "head", None),
            P("seq", "head", None),
            P("head", None),
            P("head"),
            P("head", None),
            P("head", None),
        ),
        out_specs=P("seq", "head"),
        check_vma=False,
    )
```

```python
import functools

import jax
import jax.numpy as jnp
from jax import lax
from jax.experimental import pallas as pl
from jax.experimental.pallas import tpu as pltpu
from jax.sharding import PartitionSpec as P

ITERS = 15
BLOCK = 128
F32 = jnp.float32
BF16 = jnp.bfloat16


def mm(a, b):
    return jnp.dot(a, b, preferred_element_type=F32)


def halves(value):
    high = value.astype(BF16)
    return high, (value - high.astype(F32)).astype(BF16)


def small(mebibytes):
    return pltpu.CompilerParams(vmem_limit_bytes=mebibytes * 2**20)


def state_kernel(k_ref, v_ref, gain_ref, norm_ref, state_ref, gained_ref, column_ref):
    gained = (k_ref[...].astype(F32) * gain_ref[...]).astype(BF16)
    width = gained.shape[1]
    gained_ref[...] = gained
    over_tokens = (((0,), (0,)), ((), ()))
    state_ref[0:width, :] = lax.dot_general(
        gained, gained, over_tokens, preferred_element_type=F32
    )
    state_ref[width:, :] = lax.dot_general(
        v_ref[...], gained, over_tokens, preferred_element_type=F32
    )
    column_ref[...] = jnp.broadcast_to(norm_ref[...], column_ref.shape).T


def local_state(keys, values, gain, norm_gain):
    width = keys.shape[1]
    return pl.pallas_call(
        state_kernel,
        out_shape=(
            jax.ShapeDtypeStruct((2 * width, width), F32),
            jax.ShapeDtypeStruct(keys.shape, BF16),
            jax.ShapeDtypeStruct((width, width), F32),
        ),
        name="local_state",
    )(keys, values, gain, norm_gain)


def prefix_kernel(x_ref, o_ref):
    pieces, rows = o_ref.shape[0], o_ref.shape[1]
    total = jnp.zeros(o_ref.shape[1:], F32)
    for piece in range(pieces):
        o_ref[piece] = total
        total = total + x_ref[piece]


def exclusive(pieces):
    return pl.pallas_call(
        prefix_kernel,
        out_shape=jax.ShapeDtypeStruct(pieces.shape, F32),
        compiler_params=small(2),
        name="prefix",
    )(pieces)


def solve_kernel(
    reg_ref, core_ref, q_ref, k_ref, v_ref, before_ref, column_ref, one_ref, two_ref,
    first, second, last, x_ref, r_ref, p_ref,
):
    width = q_ref.shape[1]
    blocks = q_ref.shape[0] // BLOCK
    lam = reg_ref[0]
    row = lax.broadcasted_iota(jnp.int32, (BLOCK, BLOCK), 0)
    col = lax.broadcasted_iota(jnp.int32, (BLOCK, BLOCK), 1)
    causal = row <= col
    h_state = before_ref[0:width, :]
    g_state = before_ref[width:, :]
    starts = []
    for b in range(blocks):
        rows = pl.ds(b * BLOCK, BLOCK)
        key = k_ref[rows, :]
        key_t = key.astype(F32).T.astype(BF16)
        val_t = v_ref[rows, :].astype(F32).T.astype(BF16)
        high, low = halves(h_state)
        first[b, 0:width, 0:width] = high
        first[b, 0:width, width:] = high
        first[b, width:, 0:width] = key
        first[b, width:, width:] = key
        second[b, :, 0:BLOCK] = key_t
        second[b, :, BLOCK : 2 * BLOCK] = key_t
        second[b, :, 2 * BLOCK :] = low
        high, low = halves(g_state)
        last[b, :, 0:BLOCK] = val_t
        last[b, :, BLOCK : 2 * BLOCK] = val_t
        last[b, :, 2 * BLOCK : 3 * BLOCK] = low
        last[b, :, 3 * BLOCK : 4 * BLOCK] = high
        if b + 1 < blocks:
            h_state = h_state + mm(key_t, key)
            g_state = g_state + mm(val_t, key)
        query = q_ref[rows, :].astype(F32).T
        x_ref[b] = jnp.zeros_like(query)
        r_ref[b] = query
        p_ref[b] = query
        starts.append(jnp.sum(query * query, axis=0, keepdims=True))

    def step(_, rrs):
        news = []
        for group in (range(blocks),):
            ps = {b: p_ref[b] for b in group}
            hs = {b: halves(ps[b]) for b in group}
            one = {
                b: mm(first[b], jnp.concatenate(hs[b], axis=0)) for b in group
            }
            ss = {b: halves(jnp.where(causal, one[b][width:], 0.0)) for b in group}
            two = {
                b: mm(second[b], jnp.concatenate([*ss[b], hs[b][0]], axis=0))
                for b in group
            }
            for b in group:
                p = p_ref[b]
                w = one[b][:width] + two[b] + lam * p
                rr = rrs[b]
                active = rr > 1e-30
                curve = jnp.sum(p * w, axis=0, keepdims=True)
                alpha = jnp.where(active, rr / jnp.where(active, curve, 1.0), 0.0)
                x_ref[b] = x_ref[b] + alpha * p
                r = r_ref[b] - alpha * w
                r_ref[b] = r
                new = jnp.sum(r * r, axis=0, keepdims=True)
                ratio = jnp.where(active, new / jnp.where(active, rr, 1.0), 0.0)
                p_ref[b] = r + ratio * p
                news.append(new)
        return tuple(news)

    lax.fori_loop(0, ITERS, step, tuple(starts))

    column = column_ref[...]
    rows = []
    for b in range(blocks):
        x_high, x_low = halves(x_ref[b])
        key = first[b, width:, :]
        scores = mm(key, jnp.concatenate([x_high, x_low], axis=0))
        s_high, s_low = halves(jnp.where(causal, scores, 0.0))
        read = mm(
            last[b],
            jnp.concatenate([s_high, s_low, x_high, x_high], axis=0),
        ) + mm(last[b, :, 3 * BLOCK :], x_low)
        square = jnp.mean(read * read, axis=0, keepdims=True)
        normed = read * column * lax.rsqrt(square + 1e-06)
        rows.append(normed.T.astype(BF16).astype(F32))
    half = blocks // 2
    early_first = core_ref[0] == 0
    for b in range(half):
        place = pl.ds(b * BLOCK, BLOCK)
        one_ref[place, :] = jnp.where(early_first, rows[b], rows[b + half])
        two_ref[place, :] = jnp.where(early_first, rows[b + half], rows[b])


def solve(reg, core, queries, keys, values, before, column):
    tokens, width = queries.shape
    blocks = tokens // BLOCK
    vmem = pl.BlockSpec(memory_space=pltpu.VMEM)
    return pl.pallas_call(
        solve_kernel,
        out_shape=(jax.ShapeDtypeStruct((tokens // 2, width), F32),) * 2,
        in_specs=[pl.BlockSpec(memory_space=pltpu.SMEM)] * 2 + [vmem] * 5,
        out_specs=(vmem, vmem),
        scratch_shapes=[
            pltpu.VMEM((blocks, 2 * BLOCK, 2 * width), BF16),
            pltpu.VMEM((blocks, width, 3 * BLOCK), BF16),
            pltpu.VMEM((blocks, width, 4 * BLOCK), BF16),
            pltpu.VMEM((blocks, width, BLOCK), F32),
            pltpu.VMEM((blocks, width, BLOCK), F32),
            pltpu.VMEM((blocks, width, BLOCK), F32),
        ],
        cost_estimate=pl.CostEstimate(
            flops=60 * 10**9, bytes_accessed=2**21, transcendentals=0
        ),
        compiler_params=pltpu.CompilerParams(vmem_limit_bytes=20 * 2**20),
        name="solve",
    )(reg, core, queries, keys, values, before, column)


def swapped(value):
    heads = lax.axis_size("head")
    return lax.ppermute(value, "head", [(i, i ^ 1) for i in range(heads)])


def join_weight_kernel(own_ref, other_ref, out_ref):
    chips, double, columns = out_ref.shape
    half = double // 2
    for chip in range(chips):
        here = slice(chip * columns, (chip + 1) * columns)
        out_ref[chip, 0:half, :] = own_ref[:, here]
        out_ref[chip, half:, :] = other_ref[:, here].astype(BF16)


def join_weight(own, other):
    width, columns = own.shape
    return pl.pallas_call(
        join_weight_kernel,
        out_shape=jax.ShapeDtypeStruct((columns // (2 * width), 2 * width, 2 * width), BF16),
        compiler_params=small(8),
        name="join_weight",
    )(own, other)


def open_kernel(where_ref, own_ref, other_ref, weights_ref, rows_ref, sums_ref):
    rows = jnp.concatenate([own_ref[...], other_ref[...]], axis=1).astype(BF16)
    rows_ref[...] = rows
    sums_ref[...] = mm(rows, weights_ref[where_ref[0]])


def opening(where, own, other, weights):
    tokens, width = own.shape
    vmem = pl.BlockSpec(memory_space=pltpu.VMEM)
    return pl.pallas_call(
        open_kernel,
        out_shape=(
            jax.ShapeDtypeStruct((tokens, 2 * width), BF16),
            jax.ShapeDtypeStruct((tokens, 2 * width), F32),
        ),
        in_specs=[pl.BlockSpec(memory_space=pltpu.SMEM), vmem, vmem, vmem],
        out_specs=(vmem, vmem),
        compiler_params=small(8),
        name="opening",
    )(where, own, other, weights)


def chip_ahead(away):
    chips = lax.axis_size("head") // 2
    place = lax.axis_index("head").astype(jnp.uint32)
    chip, core = lax.div(place, jnp.uint32(2)), lax.rem(place, jnp.uint32(2))
    ahead = jnp.where(core == 1, jnp.uint32(chips - away), jnp.uint32(away % chips))
    return lax.rem(chip + ahead, jnp.uint32(chips))


def project(normed, weights, core, starts):
    width = normed[0].shape[1]
    heads = lax.axis_size("head")
    far = heads // 4
    step = [2 if i % 2 == 0 else heads - 2 for i in range(heads)]
    ring = [(i, (i + step[i]) % heads) for i in range(heads)]
    cross = [(i, ((i + step[i]) % heads) ^ 1) for i in range(heads)]
    others = [swapped(normed[1]), swapped(normed[0])]
    rows, flows = [], []
    for start, own, other in zip(starts, normed, others):
        both, sums = opening(start, own, other, weights)
        rows.append(both)
        flows.append(sums)

    def part(piece, away):
        columns = lax.dynamic_index_in_dim(
            weights, chip_ahead(away), axis=0, keepdims=False
        )
        return jnp.dot(rows[piece], columns, preferred_element_type=F32)

    def own_columns(value):
        return jnp.where(core == 1, value[:, width:], value[:, :width])

    def other_columns(value):
        return jnp.where(core == 1, value[:, :width], value[:, width:])

    for away in range(far, 1, -1):
        for piece in (0, 1):
            if away - piece > 1:
                sent = lax.ppermute(flows[piece], "head", ring)
                flows[piece] = sent + part(piece, away - piece - 1)
    same, crossed = [], []
    for piece in (1, 0):
        same.append(lax.ppermute(own_columns(flows[piece]), "head", ring))
        crossed.append(lax.ppermute(other_columns(flows[piece]), "head", cross))
    first = own_columns(part(0, 0)) + same[1] + crossed[0]
    second = own_columns(part(1, 0)) + same[0] + crossed[1]
    first, second = first.astype(BF16), second.astype(BF16)
    return jnp.where(
        core == 1,
        jnp.concatenate([second, first], axis=0),
        jnp.concatenate([first, second], axis=0),
    )


def body(queries, keys, values, key_gain, reg, norm_gain, out_weight):
    width = keys.shape[2]
    devices = lax.axis_size("seq")
    key_rows, value_rows, query_rows = keys[:, 0, :], values[:, 0, :], queries[:, 0, :]
    state, gained, column = local_state(key_rows, value_rows, key_gain, norm_gain)
    rows = 2 * width // devices
    state, out_weight = lax.optimization_barrier((state, out_weight))
    parts = lax.all_to_all(state.reshape(devices, rows, width), "seq", 0, 0)
    weights = join_weight(out_weight, swapped(out_weight.astype(F32)))
    far = lax.axis_size("head") // 4
    core = lax.rem(lax.axis_index("head").astype(jnp.uint32), jnp.uint32(2))
    starts = [chip_ahead(away).astype(jnp.int32).reshape(1) for away in (far, far - 1)]
    core = core.astype(jnp.int32)
    parts, weights, core, starts = lax.optimization_barrier(
        (parts, weights, core, starts)
    )
    before = lax.all_to_all(exclusive(parts), "seq", 0, 0)
    before = before.reshape(2 * width, width)
    normed = solve(
        reg, core.reshape(1), query_rows, gained, value_rows, before, column
    )
    return project(normed, weights, core, starts)


def solution(mesh):
    return jax.shard_map(
        body,
        mesh=mesh,
        in_specs=(
            P("seq", "head", None),
            P("seq", "head", None),
            P("seq", "head", None),
            P("head", None),
            P("head"),
            P("head", None),
            P("head", None),
        ),
        out_specs=P("seq", "head"),
        check_vma=False,
    )
```

```python
import functools

import jax
import jax.numpy as jnp
from jax import lax
from jax.experimental import pallas as pl
from jax.experimental.pallas import tpu as pltpu
from jax.sharding import PartitionSpec as P

ITERS = 15
BLOCK = 128
F32 = jnp.float32
BF16 = jnp.bfloat16


def mm(a, b):
    return jnp.dot(a, b, preferred_element_type=F32)


def halves(value):
    high = value.astype(BF16)
    return high, (value - high.astype(F32)).astype(BF16)


def small(mebibytes):
    return pltpu.CompilerParams(vmem_limit_bytes=mebibytes * 2**20)


def state_kernel(k_ref, v_ref, gain_ref, norm_ref, state_ref, gained_ref, column_ref):
    gained = (k_ref[...].astype(F32) * gain_ref[...]).astype(BF16)
    width = gained.shape[1]
    gained_ref[...] = gained
    over_tokens = (((0,), (0,)), ((), ()))
    state_ref[0:width, :] = lax.dot_general(
        gained, gained, over_tokens, preferred_element_type=F32
    )
    state_ref[width:, :] = lax.dot_general(
        v_ref[...], gained, over_tokens, preferred_element_type=F32
    )
    column_ref[...] = jnp.broadcast_to(norm_ref[...], column_ref.shape).T


def local_state(keys, values, gain, norm_gain):
    width = keys.shape[1]
    return pl.pallas_call(
        state_kernel,
        out_shape=(
            jax.ShapeDtypeStruct((2 * width, width), F32),
            jax.ShapeDtypeStruct(keys.shape, BF16),
            jax.ShapeDtypeStruct((width, width), F32),
        ),
        name="local_state",
    )(keys, values, gain, norm_gain)


def prefix_kernel(x_ref, o_ref):
    pieces, rows = o_ref.shape[0], o_ref.shape[1]
    total = jnp.zeros(o_ref.shape[1:], F32)
    for piece in range(pieces):
        o_ref[piece] = total
        total = total + x_ref[piece]


def exclusive(pieces):
    return pl.pallas_call(
        prefix_kernel,
        out_shape=jax.ShapeDtypeStruct(pieces.shape, F32),
        compiler_params=small(2),
        name="prefix",
    )(pieces)


def solve_kernel(
    reg_ref, core_ref, q_ref, k_ref, v_ref, before_ref, column_ref, out_ref,
    first, second, last, x_ref, r_ref, p_ref,
):
    width = q_ref.shape[1]
    blocks = q_ref.shape[0] // BLOCK
    lam = reg_ref[0]
    row = lax.broadcasted_iota(jnp.int32, (BLOCK, BLOCK), 0)
    col = lax.broadcasted_iota(jnp.int32, (BLOCK, BLOCK), 1)
    causal = row <= col
    h_state = before_ref[0:width, :]
    g_state = before_ref[width:, :]
    starts = []
    for b in range(blocks):
        rows = pl.ds(b * BLOCK, BLOCK)
        key = k_ref[rows, :]
        key_t = key.astype(F32).T.astype(BF16)
        val_t = v_ref[rows, :].astype(F32).T.astype(BF16)
        high, low = halves(h_state)
        first[b, 0:width, 0:width] = high
        first[b, 0:width, width:] = high
        first[b, width:, 0:width] = key
        first[b, width:, width:] = key
        second[b, :, 0:BLOCK] = key_t
        second[b, :, BLOCK : 2 * BLOCK] = key_t
        second[b, :, 2 * BLOCK :] = low
        high, low = halves(g_state)
        last[b, :, 0:BLOCK] = val_t
        last[b, :, BLOCK : 2 * BLOCK] = val_t
        last[b, :, 2 * BLOCK : 3 * BLOCK] = low
        last[b, :, 3 * BLOCK : 4 * BLOCK] = high
        if b + 1 < blocks:
            h_state = h_state + mm(key_t, key)
            g_state = g_state + mm(val_t, key)
        query = q_ref[rows, :].astype(F32).T
        p_ref[b] = query
        starts.append(jnp.sum(query * query, axis=0, keepdims=True))

    rrs = starts
    for step in range(ITERS):
        begun, last_step = step > 0, step == ITERS - 1
        splits = [halves(p_ref[b]) for b in range(blocks)]
        ones = [
            mm(first[b], jnp.concatenate(splits[b], axis=0)) for b in range(blocks)
        ]
        scores = [halves(jnp.where(causal, one[width:], 0.0)) for one in ones]
        twos = [
            mm(second[b], jnp.concatenate([*scores[b], splits[b][0]], axis=0))
            for b in range(blocks)
        ]
        news = []
        for b in range(blocks):
            p, rr = p_ref[b], rrs[b]
            w = ones[b][:width] + twos[b] + lam * p
            active = rr > 1e-30
            curve = jnp.sum(p * w, axis=0, keepdims=True)
            alpha = jnp.where(active, rr / jnp.where(active, curve, 1.0), 0.0)
            x_ref[b] = x_ref[b] + alpha * p if begun else alpha * p
            if last_step:
                continue
            r = (r_ref[b] if begun else p) - alpha * w
            r_ref[b] = r
            new = jnp.sum(r * r, axis=0, keepdims=True)
            ratio = jnp.where(active, new / jnp.where(active, rr, 1.0), 0.0)
            p_ref[b] = r + ratio * p
            news.append(new)
        rrs = news

    column = column_ref[...]
    rows = []
    for b in range(blocks):
        x_high, x_low = halves(x_ref[b])
        key = first[b, width:, :]
        scores = mm(key, jnp.concatenate([x_high, x_low], axis=0))
        s_high, s_low = halves(jnp.where(causal, scores, 0.0))
        read = mm(
            last[b],
            jnp.concatenate([s_high, s_low, x_high, x_high], axis=0),
        ) + mm(last[b, :, 3 * BLOCK :], x_low)
        square = jnp.mean(read * read, axis=0, keepdims=True)
        normed = read * column * lax.rsqrt(square + 1e-06)
        rows.append(normed.T.astype(BF16).astype(F32))
    half = blocks // 2
    early_first = core_ref[0] == 0
    for b in range(half):
        one = jnp.where(early_first, rows[b], rows[b + half])
        two = jnp.where(early_first, rows[b + half], rows[b])
        out_ref[b * BLOCK : (b + 1) * BLOCK, :] = one
        out_ref[(b + half) * BLOCK : (b + half + 1) * BLOCK, :] = two


def solve(reg, core, queries, keys, values, before, column):
    tokens, width = queries.shape
    blocks = tokens // BLOCK
    vmem = pl.BlockSpec(memory_space=pltpu.VMEM)
    return pl.pallas_call(
        solve_kernel,
        out_shape=jax.ShapeDtypeStruct((tokens, width), F32),
        in_specs=[pl.BlockSpec(memory_space=pltpu.SMEM)] * 2 + [vmem] * 5,
        out_specs=vmem,
        scratch_shapes=[
            pltpu.VMEM((blocks, 2 * BLOCK, 2 * width), BF16),
            pltpu.VMEM((blocks, width, 3 * BLOCK), BF16),
            pltpu.VMEM((blocks, width, 4 * BLOCK), BF16),
            pltpu.VMEM((blocks, width, BLOCK), F32),
            pltpu.VMEM((blocks, width, BLOCK), F32),
            pltpu.VMEM((blocks, width, BLOCK), F32),
        ],
        cost_estimate=pl.CostEstimate(
            flops=60 * 10**9, bytes_accessed=2**21, transcendentals=0
        ),
        compiler_params=pltpu.CompilerParams(vmem_limit_bytes=20 * 2**20),
        name="solve",
    )(reg, core, queries, keys, values, before, column)


def swapped(value):
    heads = lax.axis_size("head")
    return lax.ppermute(value, "head", [(i, i ^ 1) for i in range(heads)])


def join_weight_kernel(own_ref, other_ref, out_ref):
    chips, double, columns = out_ref.shape
    half = double // 2
    for chip in range(chips):
        here = slice(chip * columns, (chip + 1) * columns)
        out_ref[chip, 0:half, :] = own_ref[:, here]
        out_ref[chip, half:, :] = other_ref[:, here].astype(BF16)


def join_weight(own, other):
    width, columns = own.shape
    return pl.pallas_call(
        join_weight_kernel,
        out_shape=jax.ShapeDtypeStruct((columns // (2 * width), 2 * width, 2 * width), BF16),
        compiler_params=small(8),
        name="join_weight",
    )(own, other)


def open_kernel(
    starts_ref, own_ref, other_ref, weights_ref, rows_one, rows_two, sums_one, sums_two
):
    half = own_ref.shape[0] // 2
    for piece, (rows_ref, sums_ref) in enumerate(
        ((rows_one, sums_one), (rows_two, sums_two))
    ):
        own = own_ref[piece * half : (piece + 1) * half, :]
        other = other_ref[(1 - piece) * half : (2 - piece) * half, :]
        rows = jnp.concatenate([own, other], axis=1).astype(BF16)
        rows_ref[...] = rows
        sums_ref[...] = mm(rows, weights_ref[starts_ref[piece]])


def opening(starts, own, other, weights):
    tokens, width = own.shape
    vmem = pl.BlockSpec(memory_space=pltpu.VMEM)
    rows = jax.ShapeDtypeStruct((tokens // 2, 2 * width), BF16)
    sums = jax.ShapeDtypeStruct((tokens // 2, 2 * width), F32)
    return pl.pallas_call(
        open_kernel,
        out_shape=(rows, rows, sums, sums),
        in_specs=[pl.BlockSpec(memory_space=pltpu.SMEM), vmem, vmem, vmem],
        out_specs=(vmem,) * 4,
        compiler_params=small(10),
        name="opening",
    )(starts, own, other, weights)


def chip_ahead(away):
    chips = lax.axis_size("head") // 2
    place = lax.axis_index("head").astype(jnp.uint32)
    chip, core = lax.div(place, jnp.uint32(2)), lax.rem(place, jnp.uint32(2))
    ahead = jnp.where(core == 1, jnp.uint32(chips - away), jnp.uint32(away % chips))
    return lax.rem(chip + ahead, jnp.uint32(chips))


def project(normed, weights, core, starts):
    width = normed.shape[1]
    heads = lax.axis_size("head")
    far = heads // 4
    step = [2 if i % 2 == 0 else heads - 2 for i in range(heads)]
    ring = [(i, (i + step[i]) % heads) for i in range(heads)]
    cross = [(i, ((i + step[i]) % heads) ^ 1) for i in range(heads)]
    *rows, one, two = opening(starts, normed, swapped(normed), weights)
    flows = [one, two]

    def part(piece, away):
        columns = lax.dynamic_index_in_dim(
            weights, chip_ahead(away), axis=0, keepdims=False
        )
        return jnp.dot(rows[piece], columns, preferred_element_type=F32)

    def own_columns(value):
        return jnp.where(core == 1, value[:, width:], value[:, :width])

    def other_columns(value):
        return jnp.where(core == 1, value[:, :width], value[:, width:])

    for away in range(far, 1, -1):
        for piece in (0, 1):
            flows[piece] = lax.ppermute(flows[piece], "head", ring)
            if away - piece > 1:
                flows[piece] = flows[piece] + part(piece, away - piece - 1)
    crossed = lax.ppermute(other_columns(flows[0]), "head", cross)
    same = lax.ppermute(own_columns(flows[0]), "head", ring)
    given = swapped(other_columns(flows[1]))
    first = own_columns(part(0, 0)) + same + given
    second = own_columns(part(1, 0) + flows[1]) + crossed
    first, second = first.astype(BF16), second.astype(BF16)
    return jnp.where(
        core == 1,
        jnp.concatenate([second, first], axis=0),
        jnp.concatenate([first, second], axis=0),
    )


def body(queries, keys, values, key_gain, reg, norm_gain, out_weight):
    width = keys.shape[2]
    devices = lax.axis_size("seq")
    key_rows, value_rows, query_rows = keys[:, 0, :], values[:, 0, :], queries[:, 0, :]
    state, gained, column = local_state(key_rows, value_rows, key_gain, norm_gain)
    rows = 2 * width // devices
    state, out_weight = lax.optimization_barrier((state, out_weight))
    parts = lax.all_to_all(state.reshape(devices, rows, width), "seq", 0, 0)
    weights = join_weight(out_weight, swapped(out_weight.astype(F32)))
    far = lax.axis_size("head") // 4
    core = lax.rem(lax.axis_index("head").astype(jnp.uint32), jnp.uint32(2))
    starts = jnp.stack([chip_ahead(far), chip_ahead(far - 1)]).astype(jnp.int32)
    core = core.astype(jnp.int32)
    parts, weights, core, starts = lax.optimization_barrier(
        (parts, weights, core, starts)
    )
    before = lax.all_to_all(exclusive(parts), "seq", 0, 0)
    before = before.reshape(2 * width, width)
    normed = solve(
        reg, core.reshape(1), query_rows, gained, value_rows, before, column
    )
    return project(normed, weights, core, starts)


def solution(mesh):
    return jax.shard_map(
        body,
        mesh=mesh,
        in_specs=(
            P("seq", "head", None),
            P("seq", "head", None),
            P("seq", "head", None),
            P("head", None),
            P("head"),
            P("head", None),
            P("head", None),
        ),
        out_specs=P("seq", "head"),
        check_vma=False,
    )
```

```python
import functools

import jax
import jax.numpy as jnp
from jax import lax
from jax.experimental import pallas as pl
from jax.experimental.pallas import tpu as pltpu
from jax.sharding import PartitionSpec as P

ITERS = 15
BLOCK = 128
F32 = jnp.float32
BF16 = jnp.bfloat16


def mm(a, b):
    return jnp.dot(a, b, preferred_element_type=F32)


def halves(value):
    high = value.astype(BF16)
    return high, (value - high.astype(F32)).astype(BF16)


def small(mebibytes):
    return pltpu.CompilerParams(vmem_limit_bytes=mebibytes * 2**20)


def state_kernel(k_ref, v_ref, gain_ref, norm_ref, state_ref, gained_ref, column_ref):
    gained = (k_ref[...].astype(F32) * gain_ref[...]).astype(BF16)
    width = gained.shape[1]
    gained_ref[...] = gained
    over_tokens = (((0,), (0,)), ((), ()))
    state_ref[0:width, :] = lax.dot_general(
        gained, gained, over_tokens, preferred_element_type=F32
    )
    state_ref[width:, :] = lax.dot_general(
        v_ref[...], gained, over_tokens, preferred_element_type=F32
    )
    column_ref[...] = jnp.broadcast_to(norm_ref[...], column_ref.shape).T


def local_state(keys, values, gain, norm_gain):
    width = keys.shape[1]
    return pl.pallas_call(
        state_kernel,
        out_shape=(
            jax.ShapeDtypeStruct((2 * width, width), F32),
            jax.ShapeDtypeStruct(keys.shape, BF16),
            jax.ShapeDtypeStruct((width, width), F32),
        ),
        name="local_state",
    )(keys, values, gain, norm_gain)


def prefix_kernel(x_ref, o_ref):
    pieces, rows = o_ref.shape[0], o_ref.shape[1]
    total = jnp.zeros(o_ref.shape[1:], F32)
    for piece in range(pieces):
        o_ref[piece] = total
        total = total + x_ref[piece]


def exclusive(pieces):
    return pl.pallas_call(
        prefix_kernel,
        out_shape=jax.ShapeDtypeStruct(pieces.shape, F32),
        compiler_params=small(2),
        name="prefix",
    )(pieces)


def solve_kernel(
    reg_ref, q_ref, k_ref, v_ref, before_ref, column_ref, out_ref,
    first, second, last, x_ref, r_ref, p_ref,
):
    width = q_ref.shape[1]
    blocks = q_ref.shape[0] // BLOCK
    lam = reg_ref[0]
    row = lax.broadcasted_iota(jnp.int32, (BLOCK, BLOCK), 0)
    col = lax.broadcasted_iota(jnp.int32, (BLOCK, BLOCK), 1)
    causal = row <= col
    h_state = before_ref[0:width, :]
    g_state = before_ref[width:, :]
    starts = []
    for b in range(blocks):
        rows = pl.ds(b * BLOCK, BLOCK)
        key = k_ref[rows, :]
        key_t = key.astype(F32).T.astype(BF16)
        val_t = v_ref[rows, :].astype(F32).T.astype(BF16)
        high, low = halves(h_state)
        first[b, 0:width, 0:width] = high
        first[b, 0:width, width:] = high
        first[b, width:, 0:width] = key
        first[b, width:, width:] = key
        second[b, :, 0:BLOCK] = key_t
        second[b, :, BLOCK : 2 * BLOCK] = key_t
        second[b, :, 2 * BLOCK :] = low
        high, low = halves(g_state)
        last[b, :, 0:BLOCK] = val_t
        last[b, :, BLOCK : 2 * BLOCK] = val_t
        last[b, :, 2 * BLOCK : 3 * BLOCK] = low
        last[b, :, 3 * BLOCK : 4 * BLOCK] = high
        if b + 1 < blocks:
            h_state = h_state + mm(key_t, key)
            g_state = g_state + mm(val_t, key)
        query = q_ref[rows, :].astype(F32).T
        p_ref[b] = query
        starts.append(jnp.sum(query * query, axis=0, keepdims=True))

    rrs = starts
    for step in range(ITERS):
        begun, last_step = step > 0, step == ITERS - 1
        splits = [halves(p_ref[b]) for b in range(blocks)]
        ones = [
            mm(first[b], jnp.concatenate(splits[b], axis=0)) for b in range(blocks)
        ]
        scores = [halves(jnp.where(causal, one[width:], 0.0)) for one in ones]
        twos = [
            mm(second[b], jnp.concatenate([*scores[b], splits[b][0]], axis=0))
            for b in range(blocks)
        ]
        news = []
        for b in range(blocks):
            p, rr = p_ref[b], rrs[b]
            w = ones[b][:width] + twos[b] + lam * p
            active = rr > 1e-30
            curve = jnp.sum(p * w, axis=0, keepdims=True)
            alpha = jnp.where(active, rr / jnp.where(active, curve, 1.0), 0.0)
            x_ref[b] = x_ref[b] + alpha * p if begun else alpha * p
            if last_step:
                continue
            r = (r_ref[b] if begun else p) - alpha * w
            r_ref[b] = r
            new = jnp.sum(r * r, axis=0, keepdims=True)
            ratio = jnp.where(active, new / jnp.where(active, rr, 1.0), 0.0)
            p_ref[b] = r + ratio * p
            news.append(new)
        rrs = news

    column = column_ref[...]
    for b in range(blocks):
        x_high, x_low = halves(x_ref[b])
        key = first[b, width:, :]
        scores = mm(key, jnp.concatenate([x_high, x_low], axis=0))
        s_high, s_low = halves(jnp.where(causal, scores, 0.0))
        read = mm(
            last[b],
            jnp.concatenate([s_high, s_low, x_high, x_high], axis=0),
        ) + mm(last[b, :, 3 * BLOCK :], x_low)
        square = jnp.mean(read * read, axis=0, keepdims=True)
        normed = read * column * lax.rsqrt(square + 1e-06)
        out_ref[b * BLOCK : (b + 1) * BLOCK, :] = normed.T.astype(BF16).astype(F32)


def solve(reg, queries, keys, values, before, column):
    tokens, width = queries.shape
    blocks = tokens // BLOCK
    vmem = pl.BlockSpec(memory_space=pltpu.VMEM)
    return pl.pallas_call(
        solve_kernel,
        out_shape=jax.ShapeDtypeStruct((tokens, width), F32),
        in_specs=[pl.BlockSpec(memory_space=pltpu.SMEM)] + [vmem] * 5,
        out_specs=vmem,
        scratch_shapes=[
            pltpu.VMEM((blocks, 2 * BLOCK, 2 * width), BF16),
            pltpu.VMEM((blocks, width, 3 * BLOCK), BF16),
            pltpu.VMEM((blocks, width, 4 * BLOCK), BF16),
            pltpu.VMEM((blocks, width, BLOCK), F32),
            pltpu.VMEM((blocks, width, BLOCK), F32),
            pltpu.VMEM((blocks, width, BLOCK), F32),
        ],
        cost_estimate=pl.CostEstimate(
            flops=60 * 10**9, bytes_accessed=2**21, transcendentals=0
        ),
        compiler_params=pltpu.CompilerParams(vmem_limit_bytes=20 * 2**20),
        name="solve",
    )(reg, queries, keys, values, before, column)


def swapped(value):
    heads = lax.axis_size("head")
    return lax.ppermute(value, "head", [(i, i ^ 1) for i in range(heads)])


def join_weight_kernel(core_ref, own_ref, other_ref, out_ref):
    chips, double, width = out_ref.shape
    half = double // 2
    first = core_ref[0] == 0
    for chip in range(chips):
        zero = slice(2 * chip * width, (2 * chip + 1) * width)
        one = slice((2 * chip + 1) * width, (2 * chip + 2) * width)
        out_ref[chip, 0:half, :] = jnp.where(first, own_ref[:, zero], own_ref[:, one])
        out_ref[chip, half:, :] = jnp.where(
            first, other_ref[:, zero], other_ref[:, one]
        ).astype(BF16)


def join_weight(core, own, other):
    width, columns = own.shape
    vmem = pl.BlockSpec(memory_space=pltpu.VMEM)
    return pl.pallas_call(
        join_weight_kernel,
        out_shape=jax.ShapeDtypeStruct((columns // (2 * width), 2 * width, width), BF16),
        in_specs=[pl.BlockSpec(memory_space=pltpu.SMEM), vmem, vmem],
        out_specs=vmem,
        compiler_params=small(8),
        name="join_weight",
    )(core, own, other)


def open_kernel(far_ref, own_ref, other_ref, weights_ref, rows_ref, right_ref, left_ref):
    half = own_ref.shape[0] // 2
    rows = jnp.concatenate([own_ref[...], other_ref[...]], axis=1).astype(BF16)
    rows_ref[...] = rows
    weight = weights_ref[far_ref[0]]
    right_ref[...] = mm(rows[:half], weight)
    left_ref[...] = mm(rows[half:], weight)


def opening(far, own, other, weights):
    tokens, width = own.shape
    vmem = pl.BlockSpec(memory_space=pltpu.VMEM)
    sums = jax.ShapeDtypeStruct((tokens // 2, width), F32)
    return pl.pallas_call(
        open_kernel,
        out_shape=(jax.ShapeDtypeStruct((tokens, 2 * width), BF16), sums, sums),
        in_specs=[pl.BlockSpec(memory_space=pltpu.SMEM), vmem, vmem, vmem],
        out_specs=(vmem,) * 3,
        compiler_params=small(10),
        name="opening",
    )(far, own, other, weights)


def position():
    place = lax.axis_index("head").astype(jnp.uint32)
    return lax.div(place, jnp.uint32(2)), lax.rem(place, jnp.uint32(2))


def chip_ahead(away):
    chips = lax.axis_size("head") // 2
    chip, _ = position()
    return lax.rem(chip + jnp.uint32(away % chips), jnp.uint32(chips))


def project(normed, weights, far):
    heads = lax.axis_size("head")
    half = normed.shape[0] // 2
    right = [(i, (i + 2) % heads) for i in range(heads)]
    left = [(i, (i - 2) % heads) for i in range(heads)]
    rows, ahead, behind = opening(far, normed, swapped(normed), weights)
    ahead = lax.ppermute(ahead, "head", right)
    behind = lax.ppermute(behind, "head", left)

    def part(away):
        columns = lax.dynamic_index_in_dim(
            weights, chip_ahead(away), axis=0, keepdims=False
        )
        return jnp.dot(rows, columns, preferred_element_type=F32)

    for away in range(heads // 4 - 1, 0, -1):
        to_right, to_left = part(away), part(-away)
        if ahead.shape[0] == half:
            ahead = jnp.pad(ahead, ((0, half), (0, 0)))
            behind = jnp.pad(behind, ((half, 0), (0, 0)))
        ahead = lax.ppermute(to_right + ahead, "head", right)
        behind = lax.ppermute(to_left + behind, "head", left)
    return (part(0) + ahead + behind).astype(BF16)


def body(queries, keys, values, key_gain, reg, norm_gain, out_weight):
    width = keys.shape[2]
    devices = lax.axis_size("seq")
    key_rows, value_rows, query_rows = keys[:, 0, :], values[:, 0, :], queries[:, 0, :]
    state, gained, column = local_state(key_rows, value_rows, key_gain, norm_gain)
    rows = 2 * width // devices
    state, out_weight = lax.optimization_barrier((state, out_weight))
    parts = lax.all_to_all(state.reshape(devices, rows, width), "seq", 0, 0)
    _, core = position()
    core = core.astype(jnp.int32).reshape(1)
    weights = join_weight(core, out_weight, swapped(out_weight.astype(F32)))
    far = chip_ahead(lax.axis_size("head") // 4).astype(jnp.int32).reshape(1)
    parts, weights, far = lax.optimization_barrier((parts, weights, far))
    before = lax.all_to_all(exclusive(parts), "seq", 0, 0)
    before = before.reshape(2 * width, width)
    normed = solve(reg, query_rows, gained, value_rows, before, column)
    return project(normed, weights, far)


def solution(mesh):
    return jax.shard_map(
        body,
        mesh=mesh,
        in_specs=(
            P("seq", "head", None),
            P("seq", "head", None),
            P("seq", "head", None),
            P("head", None),
            P("head"),
            P("head", None),
            P("head", None),
        ),
        out_specs=P("seq", "head"),
        check_vma=False,
    )
```

```python
import functools

import jax
import jax.numpy as jnp
from jax import lax
from jax.experimental import pallas as pl
from jax.experimental.pallas import tpu as pltpu
from jax.sharding import PartitionSpec as P

ITERS = 15
BLOCK = 128
F32 = jnp.float32
BF16 = jnp.bfloat16


def mm(a, b):
    return jnp.dot(a, b, preferred_element_type=F32)


def halves(value):
    high = value.astype(BF16)
    return high, (value - high.astype(F32)).astype(BF16)


def small(mebibytes):
    return pltpu.CompilerParams(vmem_limit_bytes=mebibytes * 2**20)


def state_kernel(k_ref, v_ref, gain_ref, norm_ref, state_ref, gained_ref, column_ref):
    gained = (k_ref[...].astype(F32) * gain_ref[...]).astype(BF16)
    width = gained.shape[1]
    gained_ref[...] = gained
    over_tokens = (((0,), (0,)), ((), ()))
    state_ref[0:width, :] = lax.dot_general(
        gained, gained, over_tokens, preferred_element_type=F32
    )
    state_ref[width:, :] = lax.dot_general(
        v_ref[...], gained, over_tokens, preferred_element_type=F32
    )
    column_ref[...] = jnp.broadcast_to(norm_ref[...], column_ref.shape).T


def local_state(keys, values, gain, norm_gain):
    width = keys.shape[1]
    return pl.pallas_call(
        state_kernel,
        out_shape=(
            jax.ShapeDtypeStruct((2 * width, width), F32),
            jax.ShapeDtypeStruct(keys.shape, BF16),
            jax.ShapeDtypeStruct((width, width), F32),
        ),
        name="local_state",
    )(keys, values, gain, norm_gain)


def near_kernel(x_ref, o_ref, totals_ref):
    total = jnp.zeros(o_ref.shape[1:], F32)
    for piece in range(o_ref.shape[0]):
        o_ref[piece] = total
        total = total + x_ref[piece]
    for copy in range(totals_ref.shape[0]):
        totals_ref[copy] = total


def near_prefix(pieces, copies):
    return pl.pallas_call(
        near_kernel,
        out_shape=(
            jax.ShapeDtypeStruct(pieces.shape, F32),
            jax.ShapeDtypeStruct((copies, *pieces.shape[1:]), F32),
        ),
        compiler_params=small(2),
        name="near_prefix",
    )(pieces)


def far_kernel(place_ref, x_ref, totals_ref, o_ref):
    earlier = jnp.zeros(o_ref.shape[1:], F32)
    for group in range(totals_ref.shape[0]):
        earlier = earlier + jnp.where(group < place_ref[0], totals_ref[group], 0.0)
    for piece in range(o_ref.shape[0]):
        o_ref[piece] = x_ref[piece] + earlier


def far_prefix(place, pieces, totals):
    vmem = pl.BlockSpec(memory_space=pltpu.VMEM)
    return pl.pallas_call(
        far_kernel,
        out_shape=jax.ShapeDtypeStruct(pieces.shape, F32),
        in_specs=[pl.BlockSpec(memory_space=pltpu.SMEM), vmem, vmem],
        out_specs=vmem,
        compiler_params=small(2),
        name="far_prefix",
    )(place, pieces, totals)


def solve_kernel(
    reg_ref, core_ref, q_ref, k_ref, v_ref, before_ref, column_ref, out_ref,
    first, second, last, x_ref, r_ref, p_ref,
):
    width = q_ref.shape[1]
    blocks = q_ref.shape[0] // BLOCK
    lam = reg_ref[0]
    row = lax.broadcasted_iota(jnp.int32, (BLOCK, BLOCK), 0)
    col = lax.broadcasted_iota(jnp.int32, (BLOCK, BLOCK), 1)
    causal = row <= col
    h_state = before_ref[0:width, :]
    g_state = before_ref[width:, :]
    starts = []
    for b in range(blocks):
        rows = pl.ds(b * BLOCK, BLOCK)
        key = k_ref[rows, :]
        key_t = key.astype(F32).T.astype(BF16)
        val_t = v_ref[rows, :].astype(F32).T.astype(BF16)
        high, low = halves(h_state)
        first[b, 0:width, 0:width] = high
        first[b, 0:width, width:] = high
        first[b, width:, 0:width] = key
        first[b, width:, width:] = key
        second[b, :, 0:BLOCK] = key_t
        second[b, :, BLOCK : 2 * BLOCK] = key_t
        second[b, :, 2 * BLOCK :] = low
        high, low = halves(g_state)
        last[b, :, 0:BLOCK] = val_t
        last[b, :, BLOCK : 2 * BLOCK] = val_t
        last[b, :, 2 * BLOCK : 3 * BLOCK] = low
        last[b, :, 3 * BLOCK : 4 * BLOCK] = high
        if b + 1 < blocks:
            h_state = h_state + mm(key_t, key)
            g_state = g_state + mm(val_t, key)
        query = q_ref[rows, :].astype(F32).T
        p_ref[b] = query
        starts.append(jnp.sum(query * query, axis=0, keepdims=True))

    rrs = starts
    for step in range(ITERS):
        begun, last_step = step > 0, step == ITERS - 1
        splits = [halves(p_ref[b]) for b in range(blocks)]
        ones = [
            mm(first[b], jnp.concatenate(splits[b], axis=0)) for b in range(blocks)
        ]
        scores = [halves(jnp.where(causal, one[width:], 0.0)) for one in ones]
        twos = [
            mm(second[b], jnp.concatenate([*scores[b], splits[b][0]], axis=0))
            for b in range(blocks)
        ]
        news = []
        for b in range(blocks):
            p, rr = p_ref[b], rrs[b]
            w = ones[b][:width] + twos[b] + lam * p
            active = rr > 1e-30
            curve = jnp.sum(p * w, axis=0, keepdims=True)
            alpha = jnp.where(active, rr / jnp.where(active, curve, 1.0), 0.0)
            x_ref[b] = x_ref[b] + alpha * p if begun else alpha * p
            if last_step:
                continue
            r = (r_ref[b] if begun else p) - alpha * w
            r_ref[b] = r
            new = jnp.sum(r * r, axis=0, keepdims=True)
            ratio = jnp.where(active, new / jnp.where(active, rr, 1.0), 0.0)
            p_ref[b] = r + ratio * p
            news.append(new)
        rrs = news

    column = column_ref[...]
    rows = []
    for b in range(blocks):
        x_high, x_low = halves(x_ref[b])
        key = first[b, width:, :]
        scores = mm(key, jnp.concatenate([x_high, x_low], axis=0))
        s_high, s_low = halves(jnp.where(causal, scores, 0.0))
        read = mm(
            last[b],
            jnp.concatenate([s_high, s_low, x_high, x_high], axis=0),
        ) + mm(last[b, :, 3 * BLOCK :], x_low)
        square = jnp.mean(read * read, axis=0, keepdims=True)
        normed = read * column * lax.rsqrt(square + 1e-06)
        rows.append(normed.T.astype(BF16).astype(F32))
    half = blocks // 2
    early_first = core_ref[0] == 0
    for b in range(half):
        one = jnp.where(early_first, rows[b], rows[b + half])
        two = jnp.where(early_first, rows[b + half], rows[b])
        out_ref[b * BLOCK : (b + 1) * BLOCK, :] = one
        out_ref[(b + half) * BLOCK : (b + half + 1) * BLOCK, :] = two


def solve(reg, core, queries, keys, values, before, column):
    tokens, width = queries.shape
    blocks = tokens // BLOCK
    vmem = pl.BlockSpec(memory_space=pltpu.VMEM)
    return pl.pallas_call(
        solve_kernel,
        out_shape=jax.ShapeDtypeStruct((tokens, width), F32),
        in_specs=[pl.BlockSpec(memory_space=pltpu.SMEM)] * 2 + [vmem] * 5,
        out_specs=vmem,
        scratch_shapes=[
            pltpu.VMEM((blocks, 2 * BLOCK, 2 * width), BF16),
            pltpu.VMEM((blocks, width, 3 * BLOCK), BF16),
            pltpu.VMEM((blocks, width, 4 * BLOCK), BF16),
            pltpu.VMEM((blocks, width, BLOCK), F32),
            pltpu.VMEM((blocks, width, BLOCK), F32),
            pltpu.VMEM((blocks, width, BLOCK), F32),
        ],
        cost_estimate=pl.CostEstimate(
            flops=60 * 10**9, bytes_accessed=2**21, transcendentals=0
        ),
        compiler_params=pltpu.CompilerParams(vmem_limit_bytes=20 * 2**20),
        name="solve",
    )(reg, core, queries, keys, values, before, column)


def swapped(value):
    heads = lax.axis_size("head")
    return lax.ppermute(value, "head", [(i, i ^ 1) for i in range(heads)])


def join_weight_kernel(own_ref, other_ref, out_ref):
    chips, double, columns = out_ref.shape
    half = double // 2
    for chip in range(chips):
        here = slice(chip * columns, (chip + 1) * columns)
        out_ref[chip, 0:half, :] = own_ref[:, here]
        out_ref[chip, half:, :] = other_ref[:, here].astype(BF16)


def join_weight(own, other):
    width, columns = own.shape
    return pl.pallas_call(
        join_weight_kernel,
        out_shape=jax.ShapeDtypeStruct((columns // (2 * width), 2 * width, 2 * width), BF16),
        compiler_params=small(8),
        name="join_weight",
    )(own, other)


def open_kernel(
    starts_ref, own_ref, other_ref, weights_ref, rows_one, rows_two, sums_one, sums_two
):
    half = own_ref.shape[0] // 2
    for piece, (rows_ref, sums_ref) in enumerate(
        ((rows_one, sums_one), (rows_two, sums_two))
    ):
        own = own_ref[piece * half : (piece + 1) * half, :]
        other = other_ref[(1 - piece) * half : (2 - piece) * half, :]
        rows = jnp.concatenate([own, other], axis=1).astype(BF16)
        rows_ref[...] = rows
        sums_ref[...] = mm(rows, weights_ref[starts_ref[piece]])


def opening(starts, own, other, weights):
    tokens, width = own.shape
    vmem = pl.BlockSpec(memory_space=pltpu.VMEM)
    rows = jax.ShapeDtypeStruct((tokens // 2, 2 * width), BF16)
    sums = jax.ShapeDtypeStruct((tokens // 2, 2 * width), F32)
    return pl.pallas_call(
        open_kernel,
        out_shape=(rows, rows, sums, sums),
        in_specs=[pl.BlockSpec(memory_space=pltpu.SMEM), vmem, vmem, vmem],
        out_specs=(vmem,) * 4,
        compiler_params=small(10),
        name="opening",
    )(starts, own, other, weights)


def chip_ahead(away):
    chips = lax.axis_size("head") // 2
    place = lax.axis_index("head").astype(jnp.uint32)
    chip, core = lax.div(place, jnp.uint32(2)), lax.rem(place, jnp.uint32(2))
    ahead = jnp.where(core == 1, jnp.uint32(chips - away), jnp.uint32(away % chips))
    return lax.rem(chip + ahead, jnp.uint32(chips))


def project(normed, weights, core, starts):
    width = normed.shape[1]
    heads = lax.axis_size("head")
    far = heads // 4
    step = [2 if i % 2 == 0 else heads - 2 for i in range(heads)]
    ring = [(i, (i + step[i]) % heads) for i in range(heads)]
    cross = [(i, ((i + step[i]) % heads) ^ 1) for i in range(heads)]
    *rows, one, two = opening(starts, normed, swapped(normed), weights)
    flows = [one, two]

    def part(piece, away):
        columns = lax.dynamic_index_in_dim(
            weights, chip_ahead(away), axis=0, keepdims=False
        )
        return jnp.dot(rows[piece], columns, preferred_element_type=F32)

    def own_columns(value):
        return jnp.where(core == 1, value[:, width:], value[:, :width])

    def other_columns(value):
        return jnp.where(core == 1, value[:, :width], value[:, width:])

    for away in range(far, 1, -1):
        for piece in (0, 1):
            flows[piece] = lax.ppermute(flows[piece], "head", ring)
            if away - piece > 1:
                flows[piece] = flows[piece] + part(piece, away - piece - 1)
    crossed = lax.ppermute(other_columns(flows[0]), "head", cross)
    same = lax.ppermute(own_columns(flows[0]), "head", ring)
    given = swapped(other_columns(flows[1]))
    first = own_columns(part(0, 0)) + same + given
    second = own_columns(part(1, 0) + flows[1]) + crossed
    first, second = first.astype(BF16), second.astype(BF16)
    return jnp.where(
        core == 1,
        jnp.concatenate([second, first], axis=0),
        jnp.concatenate([first, second], axis=0),
    )


def body(queries, keys, values, key_gain, reg, norm_gain, out_weight):
    width = keys.shape[2]
    devices = lax.axis_size("seq")
    key_rows, value_rows, query_rows = keys[:, 0, :], values[:, 0, :], queries[:, 0, :]
    state, gained, column = local_state(key_rows, value_rows, key_gain, norm_gain)
    near = min(8, devices)
    groups = devices // near
    near_groups = [[g * near + i for i in range(near)] for g in range(groups)]
    far_groups = [[g * near + i for g in range(groups)] for i in range(near)]
    rows = 2 * width // near
    state, out_weight = lax.optimization_barrier((state, out_weight))
    parts = lax.all_to_all(
        state.reshape(near, rows, width), "seq", 0, 0, axis_index_groups=near_groups
    )
    weights = join_weight(out_weight, swapped(out_weight.astype(F32)))
    far = lax.axis_size("head") // 4
    core = lax.rem(lax.axis_index("head").astype(jnp.uint32), jnp.uint32(2))
    starts = jnp.stack([chip_ahead(far), chip_ahead(far - 1)]).astype(jnp.int32)
    core = core.astype(jnp.int32)
    parts, weights, core, starts = lax.optimization_barrier(
        (parts, weights, core, starts)
    )
    place = lax.div(lax.axis_index("seq").astype(jnp.uint32), jnp.uint32(near))
    sums, totals = near_prefix(parts, groups)
    totals = lax.all_to_all(totals, "seq", 0, 0, axis_index_groups=far_groups)
    sums = far_prefix(place.astype(jnp.int32).reshape(1), sums, totals)
    before = lax.all_to_all(sums, "seq", 0, 0, axis_index_groups=near_groups)
    before = before.reshape(2 * width, width)
    normed = solve(
        reg, core.reshape(1), query_rows, gained, value_rows, before, column
    )
    return project(normed, weights, core, starts)


def solution(mesh):
    return jax.shard_map(
        body,
        mesh=mesh,
        in_specs=(
            P("seq", "head", None),
            P("seq", "head", None),
            P("seq", "head", None),
            P("head", None),
            P("head"),
            P("head", None),
            P("head", None),
        ),
        out_specs=P("seq", "head"),
        check_vma=False,
    )
```

```python
import functools

import jax
import jax.numpy as jnp
from jax import lax
from jax.experimental import pallas as pl
from jax.experimental.pallas import tpu as pltpu
from jax.sharding import PartitionSpec as P

ITERS = 15
BLOCK = 128
F32 = jnp.float32
BF16 = jnp.bfloat16


def mm(a, b):
    return jnp.dot(a, b, preferred_element_type=F32)


def halves(value):
    high = value.astype(BF16)
    return high, (value - high.astype(F32)).astype(BF16)


def small(mebibytes):
    return pltpu.CompilerParams(vmem_limit_bytes=mebibytes * 2**20)


def state_kernel(k_ref, v_ref, gain_ref, norm_ref, state_ref, gained_ref, column_ref):
    gained = (k_ref[...].astype(F32) * gain_ref[...]).astype(BF16)
    width = gained.shape[1]
    gained_ref[...] = gained
    over_tokens = (((0,), (0,)), ((), ()))
    state_ref[0:width, :] = lax.dot_general(
        gained, gained, over_tokens, preferred_element_type=F32
    )
    state_ref[width:, :] = lax.dot_general(
        v_ref[...], gained, over_tokens, preferred_element_type=F32
    )
    column_ref[...] = jnp.broadcast_to(norm_ref[...], column_ref.shape).T


def local_state(keys, values, gain, norm_gain):
    width = keys.shape[1]
    return pl.pallas_call(
        state_kernel,
        out_shape=(
            jax.ShapeDtypeStruct((2 * width, width), F32),
            jax.ShapeDtypeStruct(keys.shape, BF16),
            jax.ShapeDtypeStruct((width, width), F32),
        ),
        name="local_state",
    )(keys, values, gain, norm_gain)


def prefix_kernel(x_ref, o_ref):
    pieces, rows = o_ref.shape[0], o_ref.shape[1]
    total = jnp.zeros(o_ref.shape[1:], F32)
    for piece in range(pieces):
        o_ref[piece] = total
        total = total + x_ref[piece]


def exclusive(pieces):
    return pl.pallas_call(
        prefix_kernel,
        out_shape=jax.ShapeDtypeStruct(pieces.shape, F32),
        compiler_params=small(2),
        name="prefix",
    )(pieces)


def solve_kernel(
    reg_ref, core_ref, q_ref, k_ref, v_ref, before_ref, column_ref, out_ref,
    first, second, last, x_ref, r_ref, p_ref,
):
    width = q_ref.shape[1]
    blocks = q_ref.shape[0] // BLOCK
    lam = reg_ref[0]
    row = lax.broadcasted_iota(jnp.int32, (BLOCK, BLOCK), 0)
    col = lax.broadcasted_iota(jnp.int32, (BLOCK, BLOCK), 1)
    causal = row <= col
    h_state = before_ref[0:width, :]
    g_state = before_ref[width:, :]
    starts = []
    for b in range(blocks):
        rows = pl.ds(b * BLOCK, BLOCK)
        key = k_ref[rows, :]
        key_t = key.astype(F32).T.astype(BF16)
        val_t = v_ref[rows, :].astype(F32).T.astype(BF16)
        high, low = halves(h_state)
        first[b, 0:width, 0:width] = high
        first[b, 0:width, width:] = high
        first[b, width:, 0:width] = key
        first[b, width:, width:] = key
        second[b, :, 0:BLOCK] = key_t
        second[b, :, BLOCK : 2 * BLOCK] = key_t
        second[b, :, 2 * BLOCK :] = low
        high, low = halves(g_state)
        last[b, :, 0:BLOCK] = val_t
        last[b, :, BLOCK : 2 * BLOCK] = val_t
        last[b, :, 2 * BLOCK : 3 * BLOCK] = low
        last[b, :, 3 * BLOCK : 4 * BLOCK] = high
        if b + 1 < blocks:
            h_state = h_state + mm(key_t, key)
            g_state = g_state + mm(val_t, key)
        query = q_ref[rows, :].astype(F32).T
        p_ref[b] = query
        starts.append(jnp.sum(query * query, axis=0, keepdims=True))

    rrs = starts
    for step in range(ITERS):
        begun, last_step = step > 0, step == ITERS - 1
        splits = [halves(p_ref[b]) for b in range(blocks)]
        ones = [
            mm(first[b], jnp.concatenate(splits[b], axis=0)) for b in range(blocks)
        ]
        scores = [halves(jnp.where(causal, one[width:], 0.0)) for one in ones]
        twos = [
            mm(second[b], jnp.concatenate([*scores[b], splits[b][0]], axis=0))
            for b in range(blocks)
        ]
        news = []
        for b in range(blocks):
            p, rr = p_ref[b], rrs[b]
            w = ones[b][:width] + twos[b] + lam * p
            active = rr > 1e-30
            curve = jnp.sum(p * w, axis=0, keepdims=True)
            alpha = jnp.where(active, rr / jnp.where(active, curve, 1.0), 0.0)
            x_ref[b] = x_ref[b] + alpha * p if begun else alpha * p
            if last_step:
                continue
            r = (r_ref[b] if begun else p) - alpha * w
            r_ref[b] = r
            new = jnp.sum(r * r, axis=0, keepdims=True)
            ratio = jnp.where(active, new / jnp.where(active, rr, 1.0), 0.0)
            p_ref[b] = r + ratio * p
            news.append(new)
        rrs = news

    column = column_ref[...]
    rows = []
    for b in range(blocks):
        x_high, x_low = halves(x_ref[b])
        key = first[b, width:, :]
        scores = mm(key, jnp.concatenate([x_high, x_low], axis=0))
        s_high, s_low = halves(jnp.where(causal, scores, 0.0))
        read = mm(
            last[b],
            jnp.concatenate([s_high, s_low, x_high, x_high], axis=0),
        ) + mm(last[b, :, 3 * BLOCK :], x_low)
        square = jnp.mean(read * read, axis=0, keepdims=True)
        normed = read * column * lax.rsqrt(square + 1e-06)
        rows.append(normed.T.astype(BF16).astype(F32))
    half = blocks // 2
    early_first = core_ref[0] == 0
    for b in range(half):
        one = jnp.where(early_first, rows[b], rows[b + half])
        two = jnp.where(early_first, rows[b + half], rows[b])
        out_ref[b * BLOCK : (b + 1) * BLOCK, :] = one
        out_ref[(b + half) * BLOCK : (b + half + 1) * BLOCK, :] = two


def solve(reg, core, queries, keys, values, before, column):
    tokens, width = queries.shape
    blocks = tokens // BLOCK
    vmem = pl.BlockSpec(memory_space=pltpu.VMEM)
    return pl.pallas_call(
        solve_kernel,
        out_shape=jax.ShapeDtypeStruct((tokens, width), F32),
        in_specs=[pl.BlockSpec(memory_space=pltpu.SMEM)] * 2 + [vmem] * 5,
        out_specs=vmem,
        scratch_shapes=[
            pltpu.VMEM((blocks, 2 * BLOCK, 2 * width), BF16),
            pltpu.VMEM((blocks, width, 3 * BLOCK), BF16),
            pltpu.VMEM((blocks, width, 4 * BLOCK), BF16),
            pltpu.VMEM((blocks, width, BLOCK), F32),
            pltpu.VMEM((blocks, width, BLOCK), F32),
            pltpu.VMEM((blocks, width, BLOCK), F32),
        ],
        cost_estimate=pl.CostEstimate(
            flops=60 * 10**9, bytes_accessed=2**21, transcendentals=0
        ),
        compiler_params=pltpu.CompilerParams(vmem_limit_bytes=20 * 2**20),
        name="solve",
    )(reg, core, queries, keys, values, before, column)


def swapped(value):
    heads = lax.axis_size("head")
    return lax.ppermute(value, "head", [(i, i ^ 1) for i in range(heads)])


def widen_kernel(weight_ref, out_ref):
    out_ref[...] = weight_ref[...].astype(F32)


def widened(weight):
    return pl.pallas_call(
        widen_kernel,
        out_shape=jax.ShapeDtypeStruct(weight.shape, F32),
        cost_estimate=pl.CostEstimate(
            flops=20 * 10**9, bytes_accessed=2**21, transcendentals=0
        ),
        compiler_params=small(6),
        name="widened",
    )(weight)


def join_weight_kernel(own_ref, other_ref, out_ref):
    chips, double, columns = out_ref.shape
    half = double // 2
    for chip in range(chips):
        here = slice(chip * columns, (chip + 1) * columns)
        out_ref[chip, 0:half, :] = own_ref[:, here]
        out_ref[chip, half:, :] = other_ref[:, here].astype(BF16)


def join_weight(own, other):
    width, columns = own.shape
    return pl.pallas_call(
        join_weight_kernel,
        out_shape=jax.ShapeDtypeStruct((columns // (2 * width), 2 * width, 2 * width), BF16),
        compiler_params=small(8),
        name="join_weight",
    )(own, other)


def open_kernel(
    starts_ref, own_ref, other_ref, weights_ref, rows_one, rows_two, sums_one, sums_two
):
    half = own_ref.shape[0] // 2
    for piece, (rows_ref, sums_ref) in enumerate(
        ((rows_one, sums_one), (rows_two, sums_two))
    ):
        own = own_ref[piece * half : (piece + 1) * half, :]
        other = other_ref[(1 - piece) * half : (2 - piece) * half, :]
        rows = jnp.concatenate([own, other], axis=1).astype(BF16)
        rows_ref[...] = rows
        sums_ref[...] = mm(rows, weights_ref[starts_ref[piece]])


def opening(starts, own, other, weights):
    tokens, width = own.shape
    vmem = pl.BlockSpec(memory_space=pltpu.VMEM)
    rows = jax.ShapeDtypeStruct((tokens // 2, 2 * width), BF16)
    sums = jax.ShapeDtypeStruct((tokens // 2, 2 * width), F32)
    return pl.pallas_call(
        open_kernel,
        out_shape=(rows, rows, sums, sums),
        in_specs=[pl.BlockSpec(memory_space=pltpu.SMEM), vmem, vmem, vmem],
        out_specs=(vmem,) * 4,
        compiler_params=small(10),
        name="opening",
    )(starts, own, other, weights)


def chip_ahead(away):
    chips = lax.axis_size("head") // 2
    place = lax.axis_index("head").astype(jnp.uint32)
    chip, core = lax.div(place, jnp.uint32(2)), lax.rem(place, jnp.uint32(2))
    ahead = jnp.where(core == 1, jnp.uint32(chips - away), jnp.uint32(away % chips))
    return lax.rem(chip + ahead, jnp.uint32(chips))


def project(normed, weights, core, starts):
    width = normed.shape[1]
    heads = lax.axis_size("head")
    far = heads // 4
    step = [2 if i % 2 == 0 else heads - 2 for i in range(heads)]
    ring = [(i, (i + step[i]) % heads) for i in range(heads)]
    cross = [(i, ((i + step[i]) % heads) ^ 1) for i in range(heads)]
    *rows, one, two = opening(starts, normed, swapped(normed), weights)
    flows = [one, two]

    def part(piece, away):
        columns = lax.dynamic_index_in_dim(
            weights, chip_ahead(away), axis=0, keepdims=False
        )
        return jnp.dot(rows[piece], columns, preferred_element_type=F32)

    def own_columns(value):
        return jnp.where(core == 1, value[:, width:], value[:, :width])

    def other_columns(value):
        return jnp.where(core == 1, value[:, :width], value[:, width:])

    for away in range(far, 1, -1):
        for piece in (0, 1):
            flows[piece] = lax.ppermute(flows[piece], "head", ring)
            if away - piece > 1:
                flows[piece] = flows[piece] + part(piece, away - piece - 1)
    crossed = lax.ppermute(other_columns(flows[0]), "head", cross)
    same = lax.ppermute(own_columns(flows[0]), "head", ring)
    given = swapped(other_columns(flows[1]))
    first = own_columns(part(0, 0)) + same + given
    second = own_columns(part(1, 0) + flows[1]) + crossed
    first, second = first.astype(BF16), second.astype(BF16)
    return jnp.where(
        core == 1,
        jnp.concatenate([second, first], axis=0),
        jnp.concatenate([first, second], axis=0),
    )


def body(queries, keys, values, key_gain, reg, norm_gain, out_weight):
    width = keys.shape[2]
    devices = lax.axis_size("seq")
    key_rows, value_rows, query_rows = keys[:, 0, :], values[:, 0, :], queries[:, 0, :]
    state, gained, column = local_state(key_rows, value_rows, key_gain, norm_gain)
    rows = 2 * width // devices
    state, out_weight = lax.optimization_barrier((state, out_weight))
    parts = lax.all_to_all(state.reshape(devices, rows, width), "seq", 0, 0)
    weights = join_weight(out_weight, swapped(widened(out_weight)))
    far = lax.axis_size("head") // 4
    core = lax.rem(lax.axis_index("head").astype(jnp.uint32), jnp.uint32(2))
    starts = jnp.stack([chip_ahead(far), chip_ahead(far - 1)]).astype(jnp.int32)
    core = core.astype(jnp.int32)
    parts, weights, core, starts = lax.optimization_barrier(
        (parts, weights, core, starts)
    )
    before = lax.all_to_all(exclusive(parts), "seq", 0, 0)
    before = before.reshape(2 * width, width)
    normed = solve(
        reg, core.reshape(1), query_rows, gained, value_rows, before, column
    )
    return project(normed, weights, core, starts)


def solution(mesh):
    return jax.shard_map(
        body,
        mesh=mesh,
        in_specs=(
            P("seq", "head", None),
            P("seq", "head", None),
            P("seq", "head", None),
            P("head", None),
            P("head"),
            P("head", None),
            P("head", None),
        ),
        out_specs=P("seq", "head"),
        check_vma=False,
    )
```

```python
import functools

import jax
import jax.numpy as jnp
from jax import lax
from jax.experimental import pallas as pl
from jax.experimental.pallas import tpu as pltpu
from jax.sharding import PartitionSpec as P

ITERS = 15
BLOCK = 128
F32 = jnp.float32
BF16 = jnp.bfloat16


def mm(a, b):
    return jnp.dot(a, b, preferred_element_type=F32)


def halves(value):
    high = value.astype(BF16)
    return high, (value - high.astype(F32)).astype(BF16)


def small(mebibytes):
    return pltpu.CompilerParams(vmem_limit_bytes=mebibytes * 2**20)


def state_kernel(k_ref, v_ref, gain_ref, norm_ref, state_ref, gained_ref, column_ref):
    gained = (k_ref[...].astype(F32) * gain_ref[...]).astype(BF16)
    width = gained.shape[1]
    gained_ref[...] = gained
    over_tokens = (((0,), (0,)), ((), ()))
    state_ref[0:width, :] = lax.dot_general(
        gained, gained, over_tokens, preferred_element_type=F32
    )
    state_ref[width:, :] = lax.dot_general(
        v_ref[...], gained, over_tokens, preferred_element_type=F32
    )
    column_ref[...] = jnp.broadcast_to(norm_ref[...], column_ref.shape).T


def local_state(keys, values, gain, norm_gain):
    width = keys.shape[1]
    return pl.pallas_call(
        state_kernel,
        out_shape=(
            jax.ShapeDtypeStruct((2 * width, width), F32),
            jax.ShapeDtypeStruct(keys.shape, BF16),
            jax.ShapeDtypeStruct((width, width), F32),
        ),
        name="local_state",
    )(keys, values, gain, norm_gain)


def prefix_kernel(x_ref, o_ref):
    pieces, rows = o_ref.shape[0], o_ref.shape[1]
    total = jnp.zeros(o_ref.shape[1:], F32)
    for piece in range(pieces):
        o_ref[piece] = total
        total = total + x_ref[piece]


def exclusive(pieces):
    return pl.pallas_call(
        prefix_kernel,
        out_shape=jax.ShapeDtypeStruct(pieces.shape, F32),
        compiler_params=small(2),
        name="prefix",
    )(pieces)


def solve_kernel(
    reg_ref, core_ref, q_ref, k_ref, v_ref, before_ref, column_ref, out_ref,
    first, second, last, x_ref, r_ref, p_ref,
):
    width = q_ref.shape[1]
    blocks = q_ref.shape[0] // BLOCK
    lam = reg_ref[0]
    row = lax.broadcasted_iota(jnp.int32, (BLOCK, BLOCK), 0)
    col = lax.broadcasted_iota(jnp.int32, (BLOCK, BLOCK), 1)
    causal = row <= col
    h_state = before_ref[0:width, :]
    g_state = before_ref[width:, :]
    starts = []
    for b in range(blocks):
        rows = pl.ds(b * BLOCK, BLOCK)
        key = k_ref[rows, :]
        key_t = key.astype(F32).T.astype(BF16)
        val_t = v_ref[rows, :].astype(F32).T.astype(BF16)
        high, low = halves(h_state)
        first[b, 0:width, 0:width] = high
        first[b, 0:width, width:] = high
        first[b, width:, 0:width] = key
        first[b, width:, width:] = key
        second[b, :, 0:BLOCK] = key_t
        second[b, :, BLOCK : 2 * BLOCK] = key_t
        second[b, :, 2 * BLOCK :] = low
        high, low = halves(g_state)
        last[b, :, 0:BLOCK] = val_t
        last[b, :, BLOCK : 2 * BLOCK] = val_t
        last[b, :, 2 * BLOCK : 3 * BLOCK] = low
        last[b, :, 3 * BLOCK : 4 * BLOCK] = high
        if b + 1 < blocks:
            h_state = h_state + mm(key_t, key)
            g_state = g_state + mm(val_t, key)
        query = q_ref[rows, :].astype(F32).T
        p_ref[b] = query
        starts.append(jnp.sum(query * query, axis=0, keepdims=True))

    rrs = starts
    for step in range(ITERS):
        begun, last_step = step > 0, step == ITERS - 1
        splits = [halves(p_ref[b]) for b in range(blocks)]
        ones = [
            mm(first[b], jnp.concatenate(splits[b], axis=0)) for b in range(blocks)
        ]
        scores = [halves(jnp.where(causal, one[width:], 0.0)) for one in ones]
        twos = [
            mm(second[b], jnp.concatenate([*scores[b], splits[b][0]], axis=0))
            for b in range(blocks)
        ]
        news = []
        for b in range(blocks):
            p, rr = p_ref[b], rrs[b]
            w = ones[b][:width] + twos[b] + lam * p
            active = rr > 1e-30
            curve = jnp.sum(p * w, axis=0, keepdims=True)
            alpha = jnp.where(active, rr / jnp.where(active, curve, 1.0), 0.0)
            x_ref[b] = x_ref[b] + alpha * p if begun else alpha * p
            if last_step:
                continue
            r = (r_ref[b] if begun else p) - alpha * w
            r_ref[b] = r
            new = jnp.sum(r * r, axis=0, keepdims=True)
            ratio = jnp.where(active, new / jnp.where(active, rr, 1.0), 0.0)
            p_ref[b] = r + ratio * p
            news.append(new)
        rrs = news

    column = column_ref[...]
    rows = []
    for b in range(blocks):
        x_high, x_low = halves(x_ref[b])
        key = first[b, width:, :]
        scores = mm(key, jnp.concatenate([x_high, x_low], axis=0))
        s_high, s_low = halves(jnp.where(causal, scores, 0.0))
        read = mm(
            last[b],
            jnp.concatenate([s_high, s_low, x_high, x_high], axis=0),
        ) + mm(last[b, :, 3 * BLOCK :], x_low)
        square = jnp.mean(read * read, axis=0, keepdims=True)
        normed = read * column * lax.rsqrt(square + 1e-06)
        rows.append(normed.T.astype(BF16).astype(F32))
    half = blocks // 2
    early_first = core_ref[0] == 0
    for b in range(half):
        one = jnp.where(early_first, rows[b], rows[b + half])
        two = jnp.where(early_first, rows[b + half], rows[b])
        out_ref[b * BLOCK : (b + 1) * BLOCK, :] = one
        out_ref[(b + half) * BLOCK : (b + half + 1) * BLOCK, :] = two


def solve(reg, core, queries, keys, values, before, column):
    tokens, width = queries.shape
    blocks = tokens // BLOCK
    vmem = pl.BlockSpec(memory_space=pltpu.VMEM)
    return pl.pallas_call(
        solve_kernel,
        out_shape=jax.ShapeDtypeStruct((tokens, width), F32),
        in_specs=[pl.BlockSpec(memory_space=pltpu.SMEM)] * 2 + [vmem] * 5,
        out_specs=vmem,
        scratch_shapes=[
            pltpu.VMEM((blocks, 2 * BLOCK, 2 * width), BF16),
            pltpu.VMEM((blocks, width, 3 * BLOCK), BF16),
            pltpu.VMEM((blocks, width, 4 * BLOCK), BF16),
            pltpu.VMEM((blocks, width, BLOCK), F32),
            pltpu.VMEM((blocks, width, BLOCK), F32),
            pltpu.VMEM((blocks, width, BLOCK), F32),
        ],
        cost_estimate=pl.CostEstimate(
            flops=60 * 10**9, bytes_accessed=2**21, transcendentals=0
        ),
        compiler_params=pltpu.CompilerParams(vmem_limit_bytes=20 * 2**20),
        name="solve",
    )(reg, core, queries, keys, values, before, column)


def swapped(value):
    heads = lax.axis_size("head")
    return lax.ppermute(value, "head", [(i, i ^ 1) for i in range(heads)])


def join_weight_kernel(own_ref, other_ref, out_ref):
    chips, double, columns = out_ref.shape
    half = double // 2
    for chip in range(chips):
        here = slice(chip * columns, (chip + 1) * columns)
        out_ref[chip, 0:half, :] = own_ref[:, here]
        out_ref[chip, half:, :] = other_ref[:, here].astype(BF16)


def join_weight(own, other):
    width, columns = own.shape
    return pl.pallas_call(
        join_weight_kernel,
        out_shape=jax.ShapeDtypeStruct((columns // (2 * width), 2 * width, 2 * width), BF16),
        compiler_params=small(8),
        name="join_weight",
    )(own, other)


def open_kernel(
    starts_ref, own_ref, other_ref, weights_ref, rows_one, rows_two, sums_one, sums_two
):
    half = own_ref.shape[0] // 2
    for piece, (rows_ref, sums_ref) in enumerate(
        ((rows_one, sums_one), (rows_two, sums_two))
    ):
        own = own_ref[piece * half : (piece + 1) * half, :]
        other = other_ref[(1 - piece) * half : (2 - piece) * half, :]
        rows = jnp.concatenate([own, other], axis=1).astype(BF16)
        rows_ref[...] = rows
        sums_ref[...] = mm(rows, weights_ref[starts_ref[piece]])


def opening(starts, own, other, weights):
    tokens, width = own.shape
    vmem = pl.BlockSpec(memory_space=pltpu.VMEM)
    rows = jax.ShapeDtypeStruct((tokens // 2, 2 * width), BF16)
    sums = jax.ShapeDtypeStruct((tokens // 2, 2 * width), F32)
    return pl.pallas_call(
        open_kernel,
        out_shape=(rows, rows, sums, sums),
        in_specs=[pl.BlockSpec(memory_space=pltpu.SMEM), vmem, vmem, vmem],
        out_specs=(vmem,) * 4,
        compiler_params=small(10),
        name="opening",
    )(starts, own, other, weights)


def hop_kernel(chip_ref, sums_ref, rows_ref, weights_ref, out_ref):
    out_ref[...] = sums_ref[...] + mm(rows_ref[...], weights_ref[chip_ref[0]])


def hop(chip, sums, rows, weights):
    vmem = pl.BlockSpec(memory_space=pltpu.VMEM)
    return pl.pallas_call(
        hop_kernel,
        out_shape=jax.ShapeDtypeStruct(sums.shape, F32),
        in_specs=[pl.BlockSpec(memory_space=pltpu.SMEM), vmem, vmem, vmem],
        out_specs=vmem,
        compiler_params=small(8),
        name="hop",
    )(chip, sums, rows, weights)


def finish_kernel(core_ref, one_a, one_b, two_a, two_b, out_ref):
    half = one_a.shape[0]
    one = one_a[...] + one_b[...]
    two = two_a[...] + two_b[...]
    early_first = core_ref[0] == 0
    out_ref[0:half, :] = jnp.where(early_first, one, two).astype(BF16)
    out_ref[half:, :] = jnp.where(early_first, two, one).astype(BF16)


def finish(core, first, second):
    half, width = first[0].shape
    vmem = pl.BlockSpec(memory_space=pltpu.VMEM)
    return pl.pallas_call(
        finish_kernel,
        out_shape=jax.ShapeDtypeStruct((2 * half, width), BF16),
        in_specs=[pl.BlockSpec(memory_space=pltpu.SMEM)] + [vmem] * 4,
        out_specs=vmem,
        compiler_params=small(6),
        name="finish",
    )(core, *first, *second)


def chip_ahead(away):
    chips = lax.axis_size("head") // 2
    place = lax.axis_index("head").astype(jnp.uint32)
    chip, core = lax.div(place, jnp.uint32(2)), lax.rem(place, jnp.uint32(2))
    ahead = jnp.where(core == 1, jnp.uint32(chips - away), jnp.uint32(away % chips))
    return lax.rem(chip + ahead, jnp.uint32(chips))


def project(normed, weights, core, starts, hops):
    width = normed.shape[1]
    heads = lax.axis_size("head")
    far = heads // 4
    step = [2 if i % 2 == 0 else heads - 2 for i in range(heads)]
    ring = [(i, (i + step[i]) % heads) for i in range(heads)]
    cross = [(i, ((i + step[i]) % heads) ^ 1) for i in range(heads)]
    *rows, one, two = opening(starts, normed, swapped(normed), weights)
    flows = [one, two]

    def part(piece, away):
        columns = lax.dynamic_index_in_dim(
            weights, chip_ahead(away), axis=0, keepdims=False
        )
        return jnp.dot(rows[piece], columns, preferred_element_type=F32)

    def own_columns(value):
        return jnp.where(core == 1, value[:, width:], value[:, :width])

    def other_columns(value):
        return jnp.where(core == 1, value[:, :width], value[:, width:])

    for away in range(far, 1, -1):
        for piece in (0, 1):
            flows[piece] = lax.ppermute(flows[piece], "head", ring)
            if away - piece > 1:
                next_away = away - piece - 1
                if piece == 0:
                    flows[piece] = flows[piece] + part(piece, next_away)
                else:
                    chip = hops[next_away - 1].reshape(1)
                    flows[piece] = hop(chip, flows[piece], rows[piece], weights)
    crossed = lax.ppermute(other_columns(flows[0]), "head", cross)
    same = lax.ppermute(own_columns(flows[0]), "head", ring)
    given = swapped(other_columns(flows[1]))
    first = (own_columns(part(0, 0)) + given, same)
    second = (own_columns(part(1, 0) + flows[1]), crossed)
    return finish(core.reshape(1), first, second)


def body(queries, keys, values, key_gain, reg, norm_gain, out_weight):
    width = keys.shape[2]
    devices = lax.axis_size("seq")
    key_rows, value_rows, query_rows = keys[:, 0, :], values[:, 0, :], queries[:, 0, :]
    state, gained, column = local_state(key_rows, value_rows, key_gain, norm_gain)
    rows = 2 * width // devices
    state, out_weight = lax.optimization_barrier((state, out_weight))
    parts = lax.all_to_all(state.reshape(devices, rows, width), "seq", 0, 0)
    weights = join_weight(out_weight, swapped(out_weight.astype(F32)))
    far = lax.axis_size("head") // 4
    core = lax.rem(lax.axis_index("head").astype(jnp.uint32), jnp.uint32(2))
    starts = jnp.stack([chip_ahead(far), chip_ahead(far - 1)]).astype(jnp.int32)
    hops = [chip_ahead(away).astype(jnp.int32) for away in (1, 2)]
    core = core.astype(jnp.int32)
    parts, weights, core, starts, hops = lax.optimization_barrier(
        (parts, weights, core, starts, hops)
    )
    before = lax.all_to_all(exclusive(parts), "seq", 0, 0)
    before = before.reshape(2 * width, width)
    normed = solve(
        reg, core.reshape(1), query_rows, gained, value_rows, before, column
    )
    return project(normed, weights, core, starts, hops)


def solution(mesh):
    return jax.shard_map(
        body,
        mesh=mesh,
        in_specs=(
            P("seq", "head", None),
            P("seq", "head", None),
            P("seq", "head", None),
            P("head", None),
            P("head"),
            P("head", None),
            P("head", None),
        ),
        out_specs=P("seq", "head"),
        check_vma=False,
    )
```

```python
import functools

import jax
import jax.numpy as jnp
from jax import lax
from jax.experimental import pallas as pl
from jax.experimental.pallas import tpu as pltpu
from jax.sharding import PartitionSpec as P

ITERS = 15
BLOCK = 128
F32 = jnp.float32
BF16 = jnp.bfloat16


def mm(a, b):
    return jnp.dot(a, b, preferred_element_type=F32)


def halves(value):
    high = value.astype(BF16)
    return high, (value - high.astype(F32)).astype(BF16)


def small(mebibytes):
    return pltpu.CompilerParams(vmem_limit_bytes=mebibytes * 2**20)


def state_kernel(k_ref, v_ref, gain_ref, norm_ref, state_ref, gained_ref, column_ref):
    gained = (k_ref[...].astype(F32) * gain_ref[...]).astype(BF16)
    width = gained.shape[1]
    gained_ref[...] = gained
    over_tokens = (((0,), (0,)), ((), ()))
    state_ref[0:width, :] = lax.dot_general(
        gained, gained, over_tokens, preferred_element_type=F32
    )
    state_ref[width:, :] = lax.dot_general(
        v_ref[...], gained, over_tokens, preferred_element_type=F32
    )
    column_ref[...] = jnp.broadcast_to(norm_ref[...], column_ref.shape).T


def local_state(keys, values, gain, norm_gain):
    width = keys.shape[1]
    return pl.pallas_call(
        state_kernel,
        out_shape=(
            jax.ShapeDtypeStruct((2 * width, width), F32),
            jax.ShapeDtypeStruct(keys.shape, BF16),
            jax.ShapeDtypeStruct((width, width), F32),
        ),
        name="local_state",
    )(keys, values, gain, norm_gain)


def prefix_kernel(x_ref, o_ref):
    pieces, rows = o_ref.shape[0], o_ref.shape[1]
    total = jnp.zeros(o_ref.shape[1:], F32)
    for piece in range(pieces):
        o_ref[piece] = total
        total = total + x_ref[piece]


def exclusive(pieces):
    return pl.pallas_call(
        prefix_kernel,
        out_shape=jax.ShapeDtypeStruct(pieces.shape, F32),
        compiler_params=small(2),
        name="prefix",
    )(pieces)


def solve_kernel(
    reg_ref, core_ref, q_ref, k_ref, v_ref, before_ref, column_ref, out_ref,
    first, second, last, x_ref, r_ref, p_ref,
):
    width = q_ref.shape[1]
    blocks = q_ref.shape[0] // BLOCK
    lam = reg_ref[0]
    row = lax.broadcasted_iota(jnp.int32, (BLOCK, BLOCK), 0)
    col = lax.broadcasted_iota(jnp.int32, (BLOCK, BLOCK), 1)
    causal = row <= col
    h_state = before_ref[0:width, :]
    g_state = before_ref[width:, :]
    starts = []
    for b in range(blocks):
        rows = pl.ds(b * BLOCK, BLOCK)
        key = k_ref[rows, :]
        key_t = key.astype(F32).T.astype(BF16)
        val_t = v_ref[rows, :].astype(F32).T.astype(BF16)
        high, low = halves(h_state)
        first[b, 0:width, 0:width] = high
        first[b, 0:width, width:] = high
        first[b, width:, 0:width] = key
        first[b, width:, width:] = key
        second[b, :, 0:BLOCK] = key_t
        second[b, :, BLOCK : 2 * BLOCK] = key_t
        second[b, :, 2 * BLOCK :] = low
        high, low = halves(g_state)
        last[b, :, 0:BLOCK] = val_t
        last[b, :, BLOCK : 2 * BLOCK] = val_t
        last[b, :, 2 * BLOCK : 3 * BLOCK] = low
        last[b, :, 3 * BLOCK : 4 * BLOCK] = high
        if b + 1 < blocks:
            h_state = h_state + mm(key_t, key)
            g_state = g_state + mm(val_t, key)
        query = q_ref[rows, :].astype(F32).T
        p_ref[b] = query
        starts.append(jnp.sum(query * query, axis=0, keepdims=True))

    rrs = starts
    for step in range(ITERS):
        begun, last_step = step > 0, step == ITERS - 1
        splits = [halves(p_ref[b]) for b in range(blocks)]
        ones = [
            mm(first[b], jnp.concatenate(splits[b], axis=0)) for b in range(blocks)
        ]
        scores = [halves(jnp.where(causal, one[width:], 0.0)) for one in ones]
        twos = [
            mm(second[b], jnp.concatenate([*scores[b], splits[b][0]], axis=0))
            for b in range(blocks)
        ]
        news = []
        for b in range(blocks):
            p, rr = p_ref[b], rrs[b]
            w = ones[b][:width] + twos[b] + lam * p
            active = rr > 1e-30
            curve = jnp.sum(p * w, axis=0, keepdims=True)
            alpha = jnp.where(active, rr / jnp.where(active, curve, 1.0), 0.0)
            x_ref[b] = x_ref[b] + alpha * p if begun else alpha * p
            if last_step:
                continue
            r = (r_ref[b] if begun else p) - alpha * w
            r_ref[b] = r
            new = jnp.sum(r * r, axis=0, keepdims=True)
            ratio = jnp.where(active, new / jnp.where(active, rr, 1.0), 0.0)
            p_ref[b] = r + ratio * p
            news.append(new)
        rrs = news

    column = column_ref[...]
    rows = []
    for b in range(blocks):
        x_high, x_low = halves(x_ref[b])
        key = first[b, width:, :]
        scores = mm(key, jnp.concatenate([x_high, x_low], axis=0))
        s_high, s_low = halves(jnp.where(causal, scores, 0.0))
        read = mm(
            last[b],
            jnp.concatenate([s_high, s_low, x_high, x_high], axis=0),
        ) + mm(last[b, :, 3 * BLOCK :], x_low)
        square = jnp.mean(read * read, axis=0, keepdims=True)
        normed = read * column * lax.rsqrt(square + 1e-06)
        rows.append(normed.T.astype(BF16).astype(F32))
    half = blocks // 2
    early_first = core_ref[0] == 0
    for b in range(half):
        one = jnp.where(early_first, rows[b], rows[b + half])
        two = jnp.where(early_first, rows[b + half], rows[b])
        out_ref[b * BLOCK : (b + 1) * BLOCK, :] = one
        out_ref[(b + half) * BLOCK : (b + half + 1) * BLOCK, :] = two


def solve(reg, core, queries, keys, values, before, column):
    tokens, width = queries.shape
    blocks = tokens // BLOCK
    vmem = pl.BlockSpec(memory_space=pltpu.VMEM)
    return pl.pallas_call(
        solve_kernel,
        out_shape=jax.ShapeDtypeStruct((tokens, width), F32),
        in_specs=[pl.BlockSpec(memory_space=pltpu.SMEM)] * 2 + [vmem] * 5,
        out_specs=vmem,
        scratch_shapes=[
            pltpu.VMEM((blocks, 2 * BLOCK, 2 * width), BF16),
            pltpu.VMEM((blocks, width, 3 * BLOCK), BF16),
            pltpu.VMEM((blocks, width, 4 * BLOCK), BF16),
            pltpu.VMEM((blocks, width, BLOCK), F32),
            pltpu.VMEM((blocks, width, BLOCK), F32),
            pltpu.VMEM((blocks, width, BLOCK), F32),
        ],
        cost_estimate=pl.CostEstimate(
            flops=60 * 10**9, bytes_accessed=2**21, transcendentals=0
        ),
        compiler_params=pltpu.CompilerParams(vmem_limit_bytes=20 * 2**20),
        name="solve",
    )(reg, core, queries, keys, values, before, column)


def swapped(value):
    heads = lax.axis_size("head")
    return lax.ppermute(value, "head", [(i, i ^ 1) for i in range(heads)])


def join_weight_kernel(own_ref, other_ref, out_ref):
    chips, double, columns = out_ref.shape
    half = double // 2
    for chip in range(chips):
        here = slice(chip * columns, (chip + 1) * columns)
        out_ref[chip, 0:half, :] = own_ref[:, here]
        out_ref[chip, half:, :] = other_ref[:, here].astype(BF16)


def join_weight(own, other):
    width, columns = own.shape
    return pl.pallas_call(
        join_weight_kernel,
        out_shape=jax.ShapeDtypeStruct((columns // (2 * width), 2 * width, 2 * width), BF16),
        compiler_params=small(8),
        name="join_weight",
    )(own, other)


def open_kernel(
    starts_ref, own_ref, other_ref, weights_ref, rows_one, rows_two, sums_one, sums_two
):
    half = own_ref.shape[0] // 2
    for piece, (rows_ref, sums_ref) in enumerate(
        ((rows_one, sums_one), (rows_two, sums_two))
    ):
        own = own_ref[piece * half : (piece + 1) * half, :]
        other = other_ref[(1 - piece) * half : (2 - piece) * half, :]
        rows = jnp.concatenate([own, other], axis=1).astype(BF16)
        rows_ref[...] = rows
        sums_ref[...] = mm(rows, weights_ref[starts_ref[piece]])


def opening(starts, own, other, weights):
    tokens, width = own.shape
    vmem = pl.BlockSpec(memory_space=pltpu.VMEM)
    rows = jax.ShapeDtypeStruct((tokens // 2, 2 * width), BF16)
    sums = jax.ShapeDtypeStruct((tokens // 2, 2 * width), F32)
    return pl.pallas_call(
        open_kernel,
        out_shape=(rows, rows, sums, sums),
        in_specs=[pl.BlockSpec(memory_space=pltpu.SMEM), vmem, vmem, vmem],
        out_specs=(vmem,) * 4,
        compiler_params=small(10),
        name="opening",
    )(starts, own, other, weights)


def hop_kernel(chip_ref, sums_ref, rows_ref, weights_ref, out_ref):
    out_ref[...] = sums_ref[...] + mm(rows_ref[...], weights_ref[chip_ref[0]])


def hop(chip, sums, rows, weights):
    vmem = pl.BlockSpec(memory_space=pltpu.VMEM)
    return pl.pallas_call(
        hop_kernel,
        out_shape=jax.ShapeDtypeStruct(sums.shape, F32),
        in_specs=[pl.BlockSpec(memory_space=pltpu.SMEM), vmem, vmem, vmem],
        out_specs=vmem,
        compiler_params=small(8),
        name="hop",
    )(chip, sums, rows, weights)


def finish_kernel(core_ref, one_a, one_b, two_a, two_b, out_ref):
    half = one_a.shape[0]
    one = one_a[...] + one_b[...]
    two = two_a[...] + two_b[...]
    early_first = core_ref[0] == 0
    out_ref[0:half, :] = jnp.where(early_first, one, two).astype(BF16)
    out_ref[half:, :] = jnp.where(early_first, two, one).astype(BF16)


def finish(core, first, second):
    half, width = first[0].shape
    vmem = pl.BlockSpec(memory_space=pltpu.VMEM)
    return pl.pallas_call(
        finish_kernel,
        out_shape=jax.ShapeDtypeStruct((2 * half, width), BF16),
        in_specs=[pl.BlockSpec(memory_space=pltpu.SMEM)] + [vmem] * 4,
        out_specs=vmem,
        compiler_params=small(6),
        name="finish",
    )(core, *first, *second)


def chip_ahead(away):
    chips = lax.axis_size("head") // 2
    place = lax.axis_index("head").astype(jnp.uint32)
    chip, core = lax.div(place, jnp.uint32(2)), lax.rem(place, jnp.uint32(2))
    ahead = jnp.where(core == 1, jnp.uint32(chips - away), jnp.uint32(away % chips))
    return lax.rem(chip + ahead, jnp.uint32(chips))


def project(normed, weights, core, starts, hops):
    width = normed.shape[1]
    heads = lax.axis_size("head")
    far = heads // 4
    step = [2 if i % 2 == 0 else heads - 2 for i in range(heads)]
    ring = [(i, (i + step[i]) % heads) for i in range(heads)]
    cross = [(i, ((i + step[i]) % heads) ^ 1) for i in range(heads)]
    *rows, one, two = opening(starts, normed, swapped(normed), weights)
    flows = [one, two]

    def part(piece, away):
        columns = lax.dynamic_index_in_dim(
            weights, chip_ahead(away), axis=0, keepdims=False
        )
        return jnp.dot(rows[piece], columns, preferred_element_type=F32)

    def own_columns(value):
        return jnp.where(core == 1, value[:, width:], value[:, :width])

    def other_columns(value):
        return jnp.where(core == 1, value[:, :width], value[:, width:])

    for away in range(far, 1, -1):
        for piece in (0, 1):
            flows[piece] = lax.ppermute(flows[piece], "head", ring)
            if away - piece > 1:
                chip = hops[away - piece - 2].reshape(1)
                flows[piece] = hop(chip, flows[piece], rows[piece], weights)
    crossed = lax.ppermute(other_columns(flows[0]), "head", cross)
    same = lax.ppermute(own_columns(flows[0]), "head", ring)
    given = swapped(other_columns(flows[1]))
    first = (own_columns(part(0, 0)) + given, same)
    second = (own_columns(part(1, 0) + flows[1]), crossed)
    return finish(core.reshape(1), first, second)


def body(queries, keys, values, key_gain, reg, norm_gain, out_weight):
    width = keys.shape[2]
    devices = lax.axis_size("seq")
    key_rows, value_rows, query_rows = keys[:, 0, :], values[:, 0, :], queries[:, 0, :]
    state, gained, column = local_state(key_rows, value_rows, key_gain, norm_gain)
    rows = 2 * width // devices
    state, out_weight = lax.optimization_barrier((state, out_weight))
    parts = lax.all_to_all(state.reshape(devices, rows, width), "seq", 0, 0)
    weights = join_weight(out_weight, swapped(out_weight.astype(F32)))
    far = lax.axis_size("head") // 4
    core = lax.rem(lax.axis_index("head").astype(jnp.uint32), jnp.uint32(2))
    starts = jnp.stack([chip_ahead(far), chip_ahead(far - 1)]).astype(jnp.int32)
    hops = [chip_ahead(away).astype(jnp.int32) for away in range(1, far)]
    core = core.astype(jnp.int32)
    parts, weights, core, starts, hops = lax.optimization_barrier(
        (parts, weights, core, starts, hops)
    )
    before = lax.all_to_all(exclusive(parts), "seq", 0, 0)
    before = before.reshape(2 * width, width)
    normed = solve(
        reg, core.reshape(1), query_rows, gained, value_rows, before, column
    )
    return project(normed, weights, core, starts, hops)


def solution(mesh):
    return jax.shard_map(
        body,
        mesh=mesh,
        in_specs=(
            P("seq", "head", None),
            P("seq", "head", None),
            P("seq", "head", None),
            P("head", None),
            P("head"),
            P("head", None),
            P("head", None),
        ),
        out_specs=P("seq", "head"),
        check_vma=False,
    )
```

```python
import functools

import jax
import jax.numpy as jnp
from jax import lax
from jax.experimental import pallas as pl
from jax.experimental.pallas import tpu as pltpu
from jax.sharding import PartitionSpec as P

ITERS = 15
BLOCK = 128
F32 = jnp.float32
BF16 = jnp.bfloat16


def mm(a, b):
    return jnp.dot(a, b, preferred_element_type=F32)


def halves(value):
    high = value.astype(BF16)
    return high, (value - high.astype(F32)).astype(BF16)


def small(mebibytes):
    return pltpu.CompilerParams(vmem_limit_bytes=mebibytes * 2**20)


def state_kernel(k_ref, v_ref, gain_ref, norm_ref, state_ref, gained_ref, column_ref):
    gained = (k_ref[...].astype(F32) * gain_ref[...]).astype(BF16)
    width = gained.shape[1]
    gained_ref[...] = gained
    over_tokens = (((0,), (0,)), ((), ()))
    state_ref[0:width, :] = lax.dot_general(
        gained, gained, over_tokens, preferred_element_type=F32
    )
    state_ref[width:, :] = lax.dot_general(
        v_ref[...], gained, over_tokens, preferred_element_type=F32
    )
    column_ref[...] = jnp.broadcast_to(norm_ref[...], column_ref.shape).T


def local_state(keys, values, gain, norm_gain):
    width = keys.shape[1]
    return pl.pallas_call(
        state_kernel,
        out_shape=(
            jax.ShapeDtypeStruct((2 * width, width), F32),
            jax.ShapeDtypeStruct(keys.shape, BF16),
            jax.ShapeDtypeStruct((width, width), F32),
        ),
        name="local_state",
    )(keys, values, gain, norm_gain)


def prefix_kernel(x_ref, o_ref):
    pieces, rows = o_ref.shape[0], o_ref.shape[1]
    total = jnp.zeros(o_ref.shape[1:], F32)
    for piece in range(pieces):
        o_ref[piece] = total
        total = total + x_ref[piece]


def exclusive(pieces):
    return pl.pallas_call(
        prefix_kernel,
        out_shape=jax.ShapeDtypeStruct(pieces.shape, F32),
        compiler_params=small(2),
        name="prefix",
    )(pieces)


def solve_kernel(
    reg_ref, core_ref, q_ref, k_ref, v_ref, before_ref, column_ref, out_ref,
    first, second, last, x_ref, r_ref, p_ref,
):
    width = q_ref.shape[1]
    blocks = q_ref.shape[0] // BLOCK
    lam = reg_ref[0]
    row = lax.broadcasted_iota(jnp.int32, (BLOCK, BLOCK), 0)
    col = lax.broadcasted_iota(jnp.int32, (BLOCK, BLOCK), 1)
    causal = row <= col
    h_state = before_ref[0:width, :]
    g_state = before_ref[width:, :]
    starts = []
    for b in range(blocks):
        rows = pl.ds(b * BLOCK, BLOCK)
        key = k_ref[rows, :]
        key_t = key.astype(F32).T.astype(BF16)
        val_t = v_ref[rows, :].astype(F32).T.astype(BF16)
        high, low = halves(h_state)
        first[b, 0:width, 0:width] = high
        first[b, 0:width, width:] = high
        first[b, width:, 0:width] = key
        first[b, width:, width:] = key
        second[b, :, 0:BLOCK] = key_t
        second[b, :, BLOCK : 2 * BLOCK] = key_t
        second[b, :, 2 * BLOCK :] = low
        high, low = halves(g_state)
        last[b, :, 0:BLOCK] = val_t
        last[b, :, BLOCK : 2 * BLOCK] = val_t
        last[b, :, 2 * BLOCK : 3 * BLOCK] = low
        last[b, :, 3 * BLOCK : 4 * BLOCK] = high
        if b + 1 < blocks:
            h_state = h_state + mm(key_t, key)
            g_state = g_state + mm(val_t, key)
        query = q_ref[rows, :].astype(F32).T
        p_ref[b] = query
        starts.append(jnp.sum(query * query, axis=0, keepdims=True))

    rrs = starts
    for step in range(ITERS):
        begun, last_step = step > 0, step == ITERS - 1
        splits = [halves(p_ref[b]) for b in range(blocks)]
        ones = [
            mm(first[b], jnp.concatenate(splits[b], axis=0)) for b in range(blocks)
        ]
        scores = [halves(jnp.where(causal, one[width:], 0.0)) for one in ones]
        twos = [
            mm(second[b], jnp.concatenate([*scores[b], splits[b][0]], axis=0))
            for b in range(blocks)
        ]
        news = []
        for b in range(blocks):
            p, rr = p_ref[b], rrs[b]
            w = ones[b][:width] + twos[b] + lam * p
            active = rr > 1e-30
            curve = jnp.sum(p * w, axis=0, keepdims=True)
            alpha = jnp.where(active, rr / jnp.where(active, curve, 1.0), 0.0)
            x_ref[b] = x_ref[b] + alpha * p if begun else alpha * p
            if last_step:
                continue
            r = (r_ref[b] if begun else p) - alpha * w
            r_ref[b] = r
            new = jnp.sum(r * r, axis=0, keepdims=True)
            ratio = jnp.where(active, new / jnp.where(active, rr, 1.0), 0.0)
            p_ref[b] = r + ratio * p
            news.append(new)
        rrs = news

    column = column_ref[...]
    rows = []
    for b in range(blocks):
        x_high, x_low = halves(x_ref[b])
        key = first[b, width:, :]
        scores = mm(key, jnp.concatenate([x_high, x_low], axis=0))
        s_high, s_low = halves(jnp.where(causal, scores, 0.0))
        read = mm(
            last[b],
            jnp.concatenate([s_high, s_low, x_high, x_high], axis=0),
        ) + mm(last[b, :, 3 * BLOCK :], x_low)
        square = jnp.mean(read * read, axis=0, keepdims=True)
        normed = read * column * lax.rsqrt(square + 1e-06)
        rows.append(normed.T.astype(BF16).astype(F32))
    half = blocks // 2
    early_first = core_ref[0] == 0
    for b in range(half):
        one = jnp.where(early_first, rows[b], rows[b + half])
        two = jnp.where(early_first, rows[b + half], rows[b])
        out_ref[b * BLOCK : (b + 1) * BLOCK, :] = one
        out_ref[(b + half) * BLOCK : (b + half + 1) * BLOCK, :] = two


def solve(reg, core, queries, keys, values, before, column):
    tokens, width = queries.shape
    blocks = tokens // BLOCK
    vmem = pl.BlockSpec(memory_space=pltpu.VMEM)
    return pl.pallas_call(
        solve_kernel,
        out_shape=jax.ShapeDtypeStruct((tokens, width), F32),
        in_specs=[pl.BlockSpec(memory_space=pltpu.SMEM)] * 2 + [vmem] * 5,
        out_specs=vmem,
        scratch_shapes=[
            pltpu.VMEM((blocks, 2 * BLOCK, 2 * width), BF16),
            pltpu.VMEM((blocks, width, 3 * BLOCK), BF16),
            pltpu.VMEM((blocks, width, 4 * BLOCK), BF16),
            pltpu.VMEM((blocks, width, BLOCK), F32),
            pltpu.VMEM((blocks, width, BLOCK), F32),
            pltpu.VMEM((blocks, width, BLOCK), F32),
        ],
        cost_estimate=pl.CostEstimate(
            flops=60 * 10**9, bytes_accessed=2**21, transcendentals=0
        ),
        compiler_params=pltpu.CompilerParams(vmem_limit_bytes=20 * 2**20),
        name="solve",
    )(reg, core, queries, keys, values, before, column)


def swapped(value):
    heads = lax.axis_size("head")
    return lax.ppermute(value, "head", [(i, i ^ 1) for i in range(heads)])


def join_weight_kernel(own_ref, other_ref, out_ref):
    chips, double, columns = out_ref.shape
    half = double // 2
    for chip in range(chips):
        here = slice(chip * columns, (chip + 1) * columns)
        out_ref[chip, 0:half, :] = own_ref[:, here]
        out_ref[chip, half:, :] = other_ref[:, here].astype(BF16)


def join_weight(own, other):
    width, columns = own.shape
    return pl.pallas_call(
        join_weight_kernel,
        out_shape=jax.ShapeDtypeStruct((columns // (2 * width), 2 * width, 2 * width), BF16),
        compiler_params=small(8),
        name="join_weight",
    )(own, other)


def open_kernel(
    starts_ref, own_ref, other_ref, weights_ref, rows_one, rows_two, sums_one, sums_two
):
    half = own_ref.shape[0] // 2
    for piece, (rows_ref, sums_ref) in enumerate(
        ((rows_one, sums_one), (rows_two, sums_two))
    ):
        own = own_ref[piece * half : (piece + 1) * half, :]
        other = other_ref[(1 - piece) * half : (2 - piece) * half, :]
        rows = jnp.concatenate([own, other], axis=1).astype(BF16)
        rows_ref[...] = rows
        sums_ref[...] = mm(rows, weights_ref[starts_ref[piece]])


def opening(starts, own, other, weights):
    tokens, width = own.shape
    vmem = pl.BlockSpec(memory_space=pltpu.VMEM)
    rows = jax.ShapeDtypeStruct((tokens // 2, 2 * width), BF16)
    sums = jax.ShapeDtypeStruct((tokens // 2, 2 * width), F32)
    return pl.pallas_call(
        open_kernel,
        out_shape=(rows, rows, sums, sums),
        in_specs=[pl.BlockSpec(memory_space=pltpu.SMEM), vmem, vmem, vmem],
        out_specs=(vmem,) * 4,
        compiler_params=small(10),
        name="opening",
    )(starts, own, other, weights)


def hop_kernel(chip_ref, sums_ref, rows_ref, weights_ref, out_ref):
    out_ref[...] = sums_ref[...] + mm(rows_ref[...], weights_ref[chip_ref[0]])


def hop(chip, sums, rows, weights):
    vmem = pl.BlockSpec(memory_space=pltpu.VMEM)
    return pl.pallas_call(
        hop_kernel,
        out_shape=jax.ShapeDtypeStruct(sums.shape, F32),
        in_specs=[pl.BlockSpec(memory_space=pltpu.SMEM), vmem, vmem, vmem],
        out_specs=vmem,
        compiler_params=small(8),
        name="hop",
    )(chip, sums, rows, weights)


def turn_kernel(starts_ref, sums_ref, rows_ref, weights_ref, own_ref, other_ref):
    width = own_ref.shape[1]
    sums = sums_ref[...]
    total = sums + mm(rows_ref[...], weights_ref[starts_ref[2]])
    first = starts_ref[3] == 0
    own_ref[...] = jnp.where(first, total[:, :width], total[:, width:])
    other_ref[...] = jnp.where(first, sums[:, width:], sums[:, :width])


def turn(starts, sums, rows, weights):
    tokens, double = sums.shape
    vmem = pl.BlockSpec(memory_space=pltpu.VMEM)
    return pl.pallas_call(
        turn_kernel,
        out_shape=(jax.ShapeDtypeStruct((tokens, double // 2), F32),) * 2,
        in_specs=[pl.BlockSpec(memory_space=pltpu.SMEM), vmem, vmem, vmem],
        out_specs=(vmem, vmem),
        compiler_params=small(8),
        name="turn",
    )(starts, sums, rows, weights)


def finish_kernel(core_ref, one_a, one_b, two_a, two_b, out_ref):
    half = one_a.shape[0]
    one = one_a[...] + one_b[...]
    two = two_a[...] + two_b[...]
    early_first = core_ref[0] == 0
    out_ref[0:half, :] = jnp.where(early_first, one, two).astype(BF16)
    out_ref[half:, :] = jnp.where(early_first, two, one).astype(BF16)


def finish(core, first, second):
    half, width = first[0].shape
    vmem = pl.BlockSpec(memory_space=pltpu.VMEM)
    return pl.pallas_call(
        finish_kernel,
        out_shape=jax.ShapeDtypeStruct((2 * half, width), BF16),
        in_specs=[pl.BlockSpec(memory_space=pltpu.SMEM)] + [vmem] * 4,
        out_specs=vmem,
        compiler_params=small(6),
        name="finish",
    )(core, *first, *second)


def chip_ahead(away):
    chips = lax.axis_size("head") // 2
    place = lax.axis_index("head").astype(jnp.uint32)
    chip, core = lax.div(place, jnp.uint32(2)), lax.rem(place, jnp.uint32(2))
    ahead = jnp.where(core == 1, jnp.uint32(chips - away), jnp.uint32(away % chips))
    return lax.rem(chip + ahead, jnp.uint32(chips))


def project(normed, weights, core, starts, hops):
    width = normed.shape[1]
    heads = lax.axis_size("head")
    far = heads // 4
    step = [2 if i % 2 == 0 else heads - 2 for i in range(heads)]
    ring = [(i, (i + step[i]) % heads) for i in range(heads)]
    cross = [(i, ((i + step[i]) % heads) ^ 1) for i in range(heads)]
    *rows, one, two = opening(starts, normed, swapped(normed), weights)
    flows = [one, two]

    def part(piece, away):
        columns = lax.dynamic_index_in_dim(
            weights, chip_ahead(away), axis=0, keepdims=False
        )
        return jnp.dot(rows[piece], columns, preferred_element_type=F32)

    def own_columns(value):
        return jnp.where(core == 1, value[:, width:], value[:, :width])

    def other_columns(value):
        return jnp.where(core == 1, value[:, :width], value[:, width:])

    for away in range(far, 1, -1):
        for piece in (0, 1):
            flows[piece] = lax.ppermute(flows[piece], "head", ring)
            if away - piece > 1:
                chip = hops[away - piece - 2].reshape(1)
                flows[piece] = hop(chip, flows[piece], rows[piece], weights)
    crossed = lax.ppermute(other_columns(flows[0]), "head", cross)
    same = lax.ppermute(own_columns(flows[0]), "head", ring)
    kept, other = turn(starts, flows[1], rows[1], weights)
    given = swapped(other)
    first = (own_columns(part(0, 0)) + given, same)
    second = (kept, crossed)
    return finish(core.reshape(1), first, second)


def body(queries, keys, values, key_gain, reg, norm_gain, out_weight):
    width = keys.shape[2]
    devices = lax.axis_size("seq")
    key_rows, value_rows, query_rows = keys[:, 0, :], values[:, 0, :], queries[:, 0, :]
    state, gained, column = local_state(key_rows, value_rows, key_gain, norm_gain)
    rows = 2 * width // devices
    state, out_weight = lax.optimization_barrier((state, out_weight))
    parts = lax.all_to_all(state.reshape(devices, rows, width), "seq", 0, 0)
    weights = join_weight(out_weight, swapped(out_weight.astype(F32)))
    far = lax.axis_size("head") // 4
    core = lax.rem(lax.axis_index("head").astype(jnp.uint32), jnp.uint32(2))
    starts = [chip_ahead(far), chip_ahead(far - 1), chip_ahead(0), core]
    starts = jnp.stack(starts).astype(jnp.int32)
    hops = [chip_ahead(away).astype(jnp.int32) for away in range(1, far)]
    core = core.astype(jnp.int32)
    parts, weights, core, starts, hops = lax.optimization_barrier(
        (parts, weights, core, starts, hops)
    )
    before = lax.all_to_all(exclusive(parts), "seq", 0, 0)
    before = before.reshape(2 * width, width)
    normed = solve(
        reg, core.reshape(1), query_rows, gained, value_rows, before, column
    )
    return project(normed, weights, core, starts, hops)


def solution(mesh):
    return jax.shard_map(
        body,
        mesh=mesh,
        in_specs=(
            P("seq", "head", None),
            P("seq", "head", None),
            P("seq", "head", None),
            P("head", None),
            P("head"),
            P("head", None),
            P("head", None),
        ),
        out_specs=P("seq", "head"),
        check_vma=False,
    )
```
